128 devices in a mesh: dp: 16 (over z, y_hi, core), frame: 8 (over x, y_lo).
Axes of the slice: x: 4, y: 4 (y_hi: 2, y_lo: 2; y = y_hi * 2 + y_lo), z: 4, core: 2. Of those that a mesh axis runs over, the one named last changes fastest.
Arguments:
- clips: bfloat16 [16, 16, 64, 1152], P('dp', 'frame'), may hold values from -6 to 6
- params: bfloat16 [1152, 4608], replicated, may hold values from -0.1875 to 0.1875
- direction: bfloat16 [1152, 4608], replicated, may hold values from -0.1875 to 0.1875
Outputs:
- tangent_out: bfloat16 [16, 16, 64, 1152], P('dp', 'frame')
- gnv: float32 [1152, 4608], P(('dp', 'frame'))
The draws below stay inside these ranges and needn't reach their ends.
All inputs are finite; a program needn't handle non-finite values.
Results may differ from the reference program's by a relative error of at most 0.025.
Values may be sent and summed in bfloat16 or wider, within the bound.
A program may use at most 192 MiB of HBM per device.

```python
from functools import partial
import jax
import jax.numpy as jnp
from jax import lax

D = 1152
HD = 72
HEADS = 8
INNER = 576
PATCHES = 64
FRAMES = 16
CLIPS = 16


def strengthened(entries, key, source, target, parts, factor):
    owner, partner = [(jnp.arange(entries.shape[axis_at]) // (entries.shape[axis_at] // parts)).reshape([-1 if axis == axis_at else 1 for axis in range(entries.ndim)]) for axis_at in (source, target)]
    chosen = jax.random.permutation(key, parts)[partner]
    strong = (owner == chosen) | (owner == (partner + parts // 2) % parts)
    return jnp.where(strong, factor * entries, entries)


def block_levels(stream_key, shape, split, least, largest):
    level, own = 1.0, jax.random.fold_in(stream_key, 6)
    for position, parts in split:
        steps = jnp.exp(jax.random.uniform(jax.random.fold_in(own, position), (parts,), jnp.float32, least / len(split), largest / len(split)))
        level = level * jnp.repeat(steps, shape[position] // parts).reshape([-1 if axis == position else 1 for axis in range(len(shape))])
    return level


def gaussian(rng, extent, deviation, bound, split=(), kind=jnp.bfloat16):
    array = jax.random.normal(rng, extent, jnp.float32) * deviation
    if len(split) > 0:
        array = block_levels(rng, extent, split, -0.22, 0.18) * array
    return jnp.clip(array, min=-bound, max=bound).astype(kind)


def gaussian_with(own_key, extent, scale, most, split, heavy, held_as=jnp.bfloat16):
    result = scale * jax.random.normal(own_key, extent, jnp.float32)
    if split:
        result = result * block_levels(own_key, extent, split, -0.22, 0.18)
    return jnp.clip(strengthened(result, jax.random.fold_in(own_key, 3), *heavy), -most, most).astype(held_as)


def setup_inputs(seed: int = 0) -> dict:
    keys = jax.random.split(jax.random.key(seed), 4)
    return {
        "clips": gaussian_with(keys[0], (CLIPS, FRAMES, PATCHES, D), 1.0, 6.0, ((0, 16), (1, 8)), (0, 3, 16, 2.0)),
        "params": gaussian(keys[1], (D, 8 * INNER), D ** -0.5, 0.1875),
        "direction": gaussian(keys[2], (D, 8 * INNER), D ** -0.5, 0.1875),
    }


def layer_norm(values):
    centred = values - lax.optimization_barrier(jnp.mean(values, axis=-1, keepdims=True))
    return centred * lax.rsqrt(lax.optimization_barrier(jnp.mean(centred * centred, axis=-1, keepdims=True)) + 1e-06)

def attend(qkv, across_frames):
    lead, second, full_width = qkv.shape
    inner_width = full_width // 3
    head_count = inner_width // HD
    split_parts = qkv.astype(jnp.float32).reshape(lead, second, 3, head_count, HD)
    query_heads = split_parts[:, :, 0]
    key_heads = split_parts[:, :, 1]
    value_heads = split_parts[:, :, 2]
    if across_frames:
        scores = jnp.einsum('qphd,kphd->phqk', query_heads, key_heads, precision=lax.Precision.HIGHEST)
    else:
        scores = jnp.einsum('fqhd,fkhd->fhqk', query_heads, key_heads, precision=lax.Precision.HIGHEST)
    weights = jnp.exp(scores * HD ** (-0.5))
    rounded = (weights / lax.optimization_barrier(jnp.sum(weights, axis=-1, keepdims=True))).astype(jnp.bfloat16)
    probabilities = lax.optimization_barrier(rounded).astype(jnp.float32)
    if across_frames:
        output = jnp.einsum('phqk,kphd->qphd', probabilities, value_heads, precision=lax.Precision.HIGHEST)
    else:
        output = jnp.einsum('fhqk,fkhd->fqhd', probabilities, value_heads, precision=lax.Precision.HIGHEST)
    return output.astype(jnp.bfloat16).reshape(lead, second, inner_width)

def matmul(left, right):
    return jnp.dot(left, right, preferred_element_type=jnp.float32)

def matmul_t(left, right):
    return lax.dot_general(left, right, (((1,), (1,)), ((), ())), preferred_element_type=jnp.float32)

def contract(left, right):
    return lax.dot_general(left, right, (((0,), (0,)), ((), ())), preferred_element_type=jnp.float32)

def split_cols(matrix, inner_width):
    return (matrix[:, :3 * inner_width], matrix[:, 3 * inner_width:4 * inner_width], matrix[:, 4 * inner_width:7 * inner_width], matrix[:, 7 * inner_width:])

def reference(clips, params, direction):
    inner_width = HEADS * HD
    s_qkv, s_out, t_qkv, t_out = split_cols(params, inner_width)
    v_sqkv, v_sout, v_tqkv, v_tout = split_cols(direction, inner_width)
    loss_scale = (CLIPS * FRAMES * PATCHES) ** (-0.5)
    row_count = FRAMES * PATCHES
    spatial = partial(attend, across_frames=False)
    temporal = partial(attend, across_frames=True)

    def one_clip(summed, clip):
        flat_clip = clip.reshape(row_count, D).astype(jnp.float32)
        normed_one = layer_norm(flat_clip).astype(jnp.bfloat16)
        qkv_one = matmul(normed_one, s_qkv).astype(jnp.bfloat16)
        tan_qkv_one = matmul(normed_one, v_sqkv).astype(jnp.bfloat16)
        attn_one, tan_attn_one = jax.jvp(spatial, (qkv_one.reshape(FRAMES, PATCHES, -1),), (tan_qkv_one.reshape(FRAMES, PATCHES, -1),))
        attn_one = attn_one.reshape(row_count, inner_width)
        tan_attn_one = tan_attn_one.reshape(row_count, inner_width)
        middle = (flat_clip + matmul_t(attn_one, s_out)).astype(jnp.bfloat16)
        tan_middle = (matmul_t(tan_attn_one, s_out) + matmul_t(attn_one, v_sout)).astype(jnp.bfloat16)
        middle_f = middle.astype(jnp.float32)
        normed_f, tan_normed_f = jax.jvp(layer_norm, (middle_f,), (tan_middle.astype(jnp.float32),))
        normed_two = normed_f.astype(jnp.bfloat16)
        tan_normed_two = tan_normed_f.astype(jnp.bfloat16)
        qkv_two = matmul(normed_two, t_qkv).astype(jnp.bfloat16)
        tan_qkv_two = (matmul(tan_normed_two, t_qkv) + matmul(normed_two, v_tqkv)).astype(jnp.bfloat16)
        attn_two, tan_attn_two = jax.jvp(temporal, (qkv_two.reshape(FRAMES, PATCHES, -1),), (tan_qkv_two.reshape(FRAMES, PATCHES, -1),))
        attn_two = attn_two.reshape(row_count, inner_width)
        tan_attn_two = tan_attn_two.reshape(row_count, inner_width)
        tangent_out = (tan_middle.astype(jnp.float32) + matmul_t(tan_attn_two, t_out) + matmul_t(attn_two, v_tout)).astype(jnp.bfloat16)
        cotangent = (tangent_out.astype(jnp.float32) * loss_scale).astype(jnp.bfloat16)
        grad_attn_two = matmul(cotangent, t_out).astype(jnp.bfloat16)
        unused_two, pull_two = jax.vjp(temporal, qkv_two.reshape(FRAMES, PATCHES, -1))
        grad_qkv_two = pull_two(grad_attn_two.reshape(FRAMES, PATCHES, -1))[0].reshape(row_count, -1)
        unused_norm, pull_norm = jax.vjp(layer_norm, middle_f)
        grad_middle = (cotangent.astype(jnp.float32) + pull_norm(matmul_t(grad_qkv_two, t_qkv))[0]).astype(jnp.bfloat16)
        grad_attn_one = matmul(grad_middle, s_out).astype(jnp.bfloat16)
        unused_one, pull_one = jax.vjp(spatial, qkv_one.reshape(FRAMES, PATCHES, -1))
        grad_qkv_one = pull_one(grad_attn_one.reshape(FRAMES, PATCHES, -1))[0].reshape(row_count, -1)
        term = jnp.concatenate([contract(normed_one, grad_qkv_one), contract(grad_middle, attn_one), contract(normed_two, grad_qkv_two), contract(cotangent, attn_two)], axis=1)
        return (summed + term, tangent_out.reshape(FRAMES, PATCHES, D))
    zeros = jnp.zeros((D, 8 * inner_width), jnp.float32)
    summed, tangent_all = lax.scan(one_clip, zeros, clips)
    return (tangent_all, summed)
```

```python
import jax
import jax.numpy as jnp
from jax import lax
from jax.experimental import pallas as pl
from jax.experimental.pallas import tpu as pltpu
from jax.sharding import PartitionSpec as P

MESH = pl.DeviceIdType.MESH
F32 = jnp.float32
BF16 = jnp.bfloat16

D = 1152
HD = 72
HEADS = 8
QKV = 1792
OUT = 640
SCALE = HD ** (-0.5)

S_QKV, S_OUT, T_QKV, T_OUT = 0, 1664, 2304, 3968

HEAD_WINDOWS = [
    (h * HD, (h + 1) * HD, h * HD // 128 * 128, -(-(h + 1) * HD // 128) * 128)
    for h in range(HEADS)
]

LEFTS = ["gy_z", "h2_z", "h2_y", "h2_x", "g_x", "h1_z", "h1_y", "h1_x"]
RIGHTS = {"q1": QKV, "o1": OUT, "q2": QKV, "o2": OUT}

JOBS = [
    (14 * 128, 1024, "zxy", [(0, 512, [("gy_z", "o1", 128)]), (512, 1024, [("h2_z", "q2", 0)])]),
    (22 * 128, 896, "yzx", [(0, 896, [("h2_y", "q2", 512)])]),
    (
        29 * 128,
        896,
        "xyz",
        [
            (0, 256, [("h2_x", "q2", 1408)]),
            (256, 384, [("h2_x", "q2", 1664), ("g_x", "o2", 0)]),
            (384, 896, [("g_x", "o2", 128)]),
        ],
    ),
    (
        10 * 128,
        512,
        "zxy",
        [(0, 384, [("h1_z", "q1", 1280)]), (384, 512, [("h1_z", "q1", 1664), ("gy_z", "o1", 0)])],
    ),
    (5 * 128, 640, "yzx", [(0, 640, [("h1_y", "q1", 640)])]),
    (0, 640, "xyz", [(0, 640, [("h1_x", "q1", 0)])]),
]
N_JOBS = len(JOBS)


def row_moves(order):
    moves = []
    for z in range(4):
        for yh in range(2):
            for c in range(2):
                base = 288 * z + 144 * yh + 72 * c
                if order == "z":
                    moves.append((base, c, 144 * z + 72 * yh, 72))
                    continue
                for x in range(4):
                    if order == "x":
                        moves.append((base + 18 * x, c, 144 * x + 36 * z + 18 * yh, 18))
                        continue
                    for yl in range(2):
                        moves.append((base + 18 * x + 9 * yl, c, 144 * (2 * yh + yl) + 36 * z + 9 * x, 9))
    return moves


def second_rows(axes, second, third):
    if axes == "zxy":
        return 72 * (third // 2) + 18 * second + 9 * (third % 2)
    if axes == "yzx":
        return 36 * second + 9 * third
    return 36 * third + 9 * second


def nn(a, b):
    return jnp.dot(a, b, preferred_element_type=F32)


def nt(a, b):
    return lax.dot_general(a, b, (((1,), (1,)), ((), ())), preferred_element_type=F32)


def tn(a, b):
    return lax.dot_general(a, b, (((0,), (0,)), ((), ())), preferred_element_type=F32)


def left_64(x):
    return pltpu.roll(x, x.shape[1] - 64, 1)


def right_64(x):
    return pltpu.roll(x, 64, 1)


def lane_mask(lo, hi, a, b):
    lane = lax.broadcasted_iota(jnp.int32, (1, b - a), 1) + a
    return (lane >= lo) & (lane < hi)


def add_head(tiles, head, value):
    lo, hi, a, b = HEAD_WINDOWS[head]
    for j in range(a // 128, b // 128):
        piece = value[:, j * 128 - a : (j + 1) * 128 - a]
        mask = lane_mask(lo, hi, j * 128, (j + 1) * 128)
        old = jnp.zeros_like(piece) if tiles[j] is None else tiles[j]
        tiles[j] = jnp.where(mask, piece, old)


def attend(qkv, dqkv, kx, dkx, pn_ref, mask):
    out, tan = [None] * 5, [None] * 5
    for h in range(HEADS):
        lo, hi, a, b = HEAD_WINDOWS[h]
        lanes = jnp.where(lane_mask(lo, hi, a, b), 1.0, 0.0).astype(BF16)
        q = qkv[:, a:b] * lanes
        dq = dqkv[:, a:b] * lanes
        k, dk = kx[:, a:b], dkx[:, a:b]
        v, dv = qkv[:, 1152 + a : 1152 + b], dqkv[:, 1152 + a : 1152 + b]
        e = jnp.where(mask, jnp.exp(nt(q, k) * SCALE), 0.0)
        pn = e * (1.0 / jnp.sum(e, axis=1, keepdims=True))
        pn_ref[h] = pn
        p = pn.astype(BF16)
        ds = (nt(dq, k) + nt(q, dk)) * SCALE
        dp = (pn * (ds - jnp.sum(pn * ds, axis=1, keepdims=True))).astype(BF16)
        add_head(out, h, nn(p, v))
        add_head(tan, h, nn(dp, v) + nn(p, dv))
    return jnp.concatenate(out, axis=1), jnp.concatenate(tan, axis=1)


def attend_back(qkv, kx, pn_ref, go, grad_ref):
    gq, gk, gv = [None] * 5, [None] * 5, [None] * 5
    for h in range(HEADS):
        lo, hi, a, b = HEAD_WINDOWS[h]
        lanes = jnp.where(lane_mask(lo, hi, a, b), 1.0, 0.0).astype(BF16)
        gow = go[:, a:b]
        gp = nt(gow * lanes, qkv[:, 1152 + a : 1152 + b]).astype(BF16).astype(F32)
        pn = pn_ref[h]
        gs = (pn * (gp - jnp.sum(gp * pn, axis=1, keepdims=True)) * SCALE).astype(BF16)
        add_head(gq, h, nn(gs, kx[:, a:b]))
        add_head(gk, h, tn(gs, qkv[:, a:b]))
        add_head(gv, h, tn(pn.astype(BF16), gow))
    gkr = right_64(jnp.concatenate(gk, axis=1))
    for j in range(4):
        grad_ref[:, j * 128 : (j + 1) * 128] = gq[j].astype(BF16)
    grad_ref[:, 512:640] = (gq[4] + gkr[:, :128]).astype(BF16)
    grad_ref[:, 640:1152] = gkr[:, 128:].astype(BF16)
    for j in range(5):
        grad_ref[:, 1152 + j * 128 : 1280 + j * 128] = gv[j].astype(BF16)


def norm_parts(x):
    centred = x - jnp.mean(x, axis=-1, keepdims=True)
    rstd = lax.rsqrt(jnp.mean(centred * centred, axis=-1, keepdims=True) + 1e-06)
    return centred * rstd, rstd


def norm_tangent(normed, rstd, dx):
    return rstd * (
        dx
        - jnp.mean(dx, axis=-1, keepdims=True)
        - normed * jnp.mean(normed * dx, axis=-1, keepdims=True)
    )


def shape_list():
    v = pltpu.VMEM
    dma = pltpu.SemaphoreType.DMA
    scratch = {
        "wp": v((D, 4608), BF16),
        "wd": v((D, 4608), BF16),
        "h1": v((128, D), BF16),
        "qkv1": v((128, QKV), BF16),
        "dqkv1": v((128, QKV), BF16),
        "kx1": v((128, OUT), BF16),
        "dkx": v((128, OUT), BF16),
        "pn1": v((HEADS, 128, 128), F32),
        "qkv2": v((128, QKV), BF16),
        "dqkv2": v((128, QKV), BF16),
        "kx2": v((128, OUT), BF16),
        "pn2": v((HEADS, 128, 128), F32),
        "go": v((128, OUT), BF16),
        "clips_s": v((8, 16, D), BF16),
        "clips_r": v((8, 16, D), BF16),
        "attn_s": v((8, 16, 2 * OUT), BF16),
        "attn_r": v((8, 16, 2 * OUT), BF16),
        "go_s": v((8, 16, OUT), BF16),
        "go_r": v((8, 16, OUT), BF16),
        "tan_s": v((8, 16, D), BF16),
        "tan_r": v((8, 16, D), BF16),
        "lt": v((D, 128), F32),
        "lts": v((2, 576, 128), F32),
        "left": v((len(LEFTS), 576, 256), BF16),
        "left_s": v((len(LEFTS), 576, 128), BF16),
    }
    for name, width in RIGHTS.items():
        scratch["r_" + name] = v((256, width), BF16)
    for i, (_, n, _, _) in enumerate(JOBS):
        scratch[f"p{i}"] = v((4, 144, n), BF16)
        scratch[f"v{i}"] = v((3, 144, n), BF16)
        scratch[f"s2_{i}"] = v((4, 48, n), BF16)
        scratch[f"v2_{i}"] = v((3, 48, n), BF16)
        scratch[f"s3_{i}"] = v((4, 16, n), BF16)
        scratch[f"v3_{i}"] = v((3, 16, n), BF16)
    scratch["acc1"] = v((144, 1024), F32)
    scratch["acc2"] = v((48, 1024), F32)
    scratch["pad2"] = v((48, 1024), F32)
    scratch["pad3"] = v((16, 1024), F32)
    scratch["w_sem"] = dma((8,))
    scratch["a_send"] = dma((4, 7))
    scratch["a_recv"] = dma((4, 7))
    scratch["c_send"] = dma((len(LEFTS) + len(RIGHTS),))
    scratch["c_recv"] = dma((len(LEFTS) + len(RIGHTS),))
    scratch["rs_send"] = dma((N_JOBS, 3, 3))
    scratch["rs_recv"] = dma((N_JOBS, 3, 3))
    return scratch


SCRATCH = shape_list()


def kernel(clips_ref, params_ref, direction_ref, tan_ref, gnv_ref, *scratch_refs):
    s = dict(zip(SCRATCH, scratch_refs))
    dp, fr = lax.axis_index("dp"), lax.axis_index("frame")
    core, y_hi, z = dp % 2, dp // 2 % 2, dp // 4
    x, y_lo = fr // 2, fr % 2
    where = {"z": z, "y": 2 * y_hi + y_lo, "x": x}

    def device(at, c):
        return (at["z"] * 4 + at["y"] // 2 * 2 + c, at["x"] * 2 + at["y"] % 2)

    def along(axis, k):
        at = dict(where)
        at[axis] = (at[axis] + k) % 4
        return device(at, core)

    partner = (dp + 1 - 2 * core, fr)

    def remote(src, dst, send, recv, to):
        copy = pltpu.make_async_remote_copy(
            src_ref=src, dst_ref=dst, send_sem=send, recv_sem=recv, device_id=to, device_id_type=MESH
        )
        copy.start()
        sent.append(copy)
        return copy

    sent = []

    loads = []
    for i, (lo, hi) in enumerate([(0, 1792), (1792, 2304), (2304, 4096), (4096, 4608)]):
        pair = []
        for j, (src, dst) in enumerate([(params_ref, s["wp"]), (direction_ref, s["wd"])]):
            copy = pltpu.make_async_copy(src.at[:, lo:hi], dst.at[:, lo:hi], s["w_sem"].at[2 * i + j])
            copy.start()
            pair.append(copy)
        loads.append(pair)

    def loaded(i):
        for copy in loads[i]:
            copy.wait()

    barrier = pltpu.get_barrier_semaphore()
    peers = [along(axis, k) for axis in "zyx" for k in (1, 2, 3)]
    peers += [(dp, (x + k) % 4 * 2 + 1 - y_lo) for k in (1, 2, 3)]
    peers.append(partner)
    for peer in peers:
        pl.semaphore_signal(barrier, inc=1, device_id=peer, device_id_type=MESH)

    natural = clips_ref[...].astype(F32)
    tokens = jnp.concatenate(
        [natural[f, 8 * t : 8 * t + 8] for t in range(8) for f in range(2)], axis=0
    )
    s["clips_s"][...] = tokens.astype(BF16).reshape(8, 16, D)
    h1f, _ = norm_parts(tokens)
    s["h1"][...] = h1f.astype(BF16)

    pl.semaphore_wait(barrier, len(peers))

    def frame_exchange(which, src, dst):
        copies = []
        for k in range(1, 8):
            t = (fr + k) % 8
            copies.append(
                remote(src.at[t], dst.at[fr], s["a_send"].at[which, k - 1], s["a_recv"].at[which, k - 1], (dp, t))
            )
        dst[fr] = src[fr]
        return copies

    def arrived(copies):
        for copy in copies:
            copy.wait_recv()

    clips_copies = frame_exchange(0, s["clips_s"], s["clips_r"])

    left_copies = {}

    def prepare_left(value, names):
        s["lt"][...] = value.T
        for name in names:
            i = LEFTS.index(name)
            for src, c, dst, rows in row_moves(name[-1]):
                s["lts"][c, dst : dst + rows, :] = s["lt"][src : src + rows, :]
            s["left"][i, :, 0:128] = s["lts"][core].astype(BF16)
            s["left_s"][i] = s["lts"][1 - core].astype(BF16)
            left_copies[name] = remote(
                s["left_s"].at[i], s["left"].at[i, :, pl.ds(128, 128)], s["c_send"].at[i], s["c_recv"].at[i], partner
            )

    right_copies = {}

    def share_right(name):
        i = len(LEFTS) + list(RIGHTS).index(name)
        ref = s["r_" + name]
        right_copies[name] = remote(
            ref.at[pl.ds(0, 128)], ref.at[pl.ds(128, 128)], s["c_send"].at[i], s["c_recv"].at[i], partner
        )

    loaded(0)
    for lo in range(0, QKV, 256):
        s["qkv1"][:, lo : lo + 256] = nn(s["h1"][...], s["wp"][:, lo : lo + 256]).astype(BF16)
        s["dqkv1"][:, lo : lo + 256] = nn(s["h1"][...], s["wd"][:, lo : lo + 256]).astype(BF16)

    def align_keys(qkv, kx):
        kx[...] = left_64(qkv[:, 512:1152].astype(F32)).astype(BF16)

    row = lax.broadcasted_iota(jnp.int32, (128, 128), 0)
    col = lax.broadcasted_iota(jnp.int32, (128, 128), 1)
    same_frame = row // 8 % 2 == col // 8 % 2
    same_patch = row % 8 == col % 8
    align_keys(s["qkv1"], s["kx1"])
    align_keys(s["dqkv1"], s["dkx"])
    o1, do1 = attend(s["qkv1"], s["dqkv1"], s["kx1"], s["dkx"], s["pn1"], same_frame)
    s["attn_s"][:, :, 0:OUT] = right_64(o1).astype(BF16).reshape(8, 16, OUT)
    s["attn_s"][:, :, OUT:] = right_64(do1).astype(BF16).reshape(8, 16, OUT)
    attn_copies = frame_exchange(1, s["attn_s"], s["attn_r"])

    prepare_left(h1f.astype(BF16).astype(F32), ["h1_z", "h1_y", "h1_x"])

    arrived(clips_copies)
    loaded(1)
    arrived(attn_copies)
    clips_p = s["clips_r"][...].reshape(128, D).astype(F32)
    o1x = s["attn_r"][:, :, 0:OUT].reshape(128, OUT)
    do1x = s["attn_r"][:, :, OUT:].reshape(128, OUT)
    s["r_o1"][0:128, :] = o1x
    share_right("o1")
    s_out, v_sout = s["wp"][:, S_OUT : S_OUT + OUT], s["wd"][:, S_OUT : S_OUT + OUT]
    y = (clips_p + nt(o1x, s_out)).astype(BF16).astype(F32)
    dy = (nt(do1x, s_out) + nt(o1x, v_sout)).astype(BF16).astype(F32)
    h2f, rstd = norm_parts(y)
    h2 = h2f.astype(BF16)
    dh2 = norm_tangent(h2f, rstd, dy).astype(BF16)
    loaded(2)
    for lo in range(0, QKV, 256):
        wp = s["wp"][:, T_QKV + lo : T_QKV + lo + 256]
        wd = s["wd"][:, T_QKV + lo : T_QKV + lo + 256]
        s["qkv2"][:, lo : lo + 256] = nn(h2, wp).astype(BF16)
        s["dqkv2"][:, lo : lo + 256] = (nn(dh2, wp) + nn(h2, wd)).astype(BF16)
    align_keys(s["qkv2"], s["kx2"])
    align_keys(s["dqkv2"], s["dkx"])
    o2, do2 = attend(s["qkv2"], s["dqkv2"], s["kx2"], s["dkx"], s["pn2"], same_patch)
    o2x, do2x = right_64(o2).astype(BF16), right_64(do2).astype(BF16)
    s["r_o2"][0:128, :] = o2x
    share_right("o2")
    loaded(3)
    t_out, v_tout = s["wp"][:, T_OUT : T_OUT + OUT], s["wd"][:, T_OUT : T_OUT + OUT]
    tangent = (dy + nt(do2x, t_out) + nt(o2x, v_tout)).astype(BF16)
    s["tan_s"][...] = tangent.reshape(8, 16, D)
    tan_copies = frame_exchange(3, s["tan_s"], s["tan_r"])
    g = (tangent.astype(F32) * (16384 ** (-0.5))).astype(BF16)
    s["go"][...] = left_64(nn(g, t_out)).astype(BF16)
    attend_back(s["qkv2"], s["kx2"], s["pn2"], s["go"], s["r_q2"].at[pl.ds(0, 128)])
    share_right("q2")
    gq2 = s["r_q2"][0:128, :]
    gh2 = nt(gq2, s["wp"][:, T_QKV : T_QKV + QKV])
    gy = (g.astype(F32) + norm_tangent(h2f, rstd, gh2)).astype(BF16)
    s["go_s"][...] = nn(gy, s_out).astype(BF16).reshape(8, 16, OUT)
    go_copies = frame_exchange(2, s["go_s"], s["go_r"])
    prepare_left(gy.astype(F32), ["gy_z"])
    prepare_left(h2.astype(F32), ["h2_z", "h2_y", "h2_x"])
    prepare_left(g.astype(F32), ["g_x"])

    arrived(tan_copies)
    tan = s["tan_r"][...].reshape(128, D).astype(F32)
    for f in range(2):
        tan_ref[f] = jnp.concatenate(
            [tan[16 * t + 8 * f : 16 * t + 8 * f + 8] for t in range(8)], axis=0
        ).astype(BF16)
    arrived(go_copies)
    s["go"][...] = left_64(s["go_r"][...].reshape(128, OUT).astype(F32)).astype(BF16)
    attend_back(s["qkv1"], s["kx1"], s["pn1"], s["go"], s["r_q1"].at[pl.ds(0, 128)])
    share_right("q1")

    for copy in left_copies.values():
        copy.wait_recv()
    for copy in right_copies.values():
        copy.wait_recv()

    def scatter(job, stage, src, dst):
        axis = JOBS[job][2][stage]
        copies = []
        for k in (1, 2, 3):
            t = (where[axis] + k) % 4
            copies.append(
                remote(
                    src.at[t],
                    dst.at[k - 1],
                    s["rs_send"].at[job, stage, k - 1],
                    s["rs_recv"].at[job, stage, k - 1],
                    along(axis, k),
                )
            )
        return copies

    def total(job, stage, src, dst):
        mine = src[where[JOBS[job][2][stage]]].astype(F32)
        return mine + dst[0].astype(F32) + dst[1].astype(F32) + dst[2].astype(F32)

    s["pad2"][...] = jnp.zeros_like(s["pad2"])
    s["pad3"][...] = jnp.zeros_like(s["pad3"])
    flight = []
    for job, (_, n, _, segments) in enumerate(JOBS):
        for lo, hi, terms in segments:
            acc = None
            for left, right, at in terms:
                term = nn(s["left"][LEFTS.index(left)], s["r_" + right][:, at : at + hi - lo])
                acc = term if acc is None else acc + term
            s[f"p{job}"][:, :, lo:hi] = acc.astype(BF16).reshape(4, 144, hi - lo)
        flight.append(scatter(job, 0, s[f"p{job}"], s[f"v{job}"]))

    for job, (_, n, axes, _) in enumerate(JOBS):
        arrived(flight[job])
        s["acc1"][:, :n] = total(job, 0, s[f"p{job}"], s[f"v{job}"])
        for second in range(4):
            for third in range(4):
                at = second_rows(axes, second, third)
                s["pad2"][9 * third : 9 * third + 9, :n] = s["acc1"][at : at + 9, :n]
            s[f"s2_{job}"][second] = s["pad2"][:, :n].astype(BF16)
        flight[job] = scatter(job, 1, s[f"s2_{job}"], s[f"v2_{job}"])

    for job, (_, n, _, _) in enumerate(JOBS):
        arrived(flight[job])
        s["acc2"][:, :n] = total(job, 1, s[f"s2_{job}"], s[f"v2_{job}"])
        for third in range(4):
            s["pad3"][0:9, :n] = s["acc2"][9 * third : 9 * third + 9, :n]
            s[f"s3_{job}"][third] = s["pad3"][:, :n].astype(BF16)
        flight[job] = scatter(job, 2, s[f"s3_{job}"], s[f"v3_{job}"])

    for job, (first, n, _, _) in enumerate(JOBS):
        arrived(flight[job])
        gnv_ref[:, first : first + n] = total(job, 2, s[f"s3_{job}"], s[f"v3_{job}"])[0:9]

    for copy in sent:
        copy.wait_send()


def body(clips, params, direction):
    tangent, gnv = pl.pallas_call(
        kernel,
        out_shape=(
            jax.ShapeDtypeStruct((2, 64, D), BF16),
            jax.ShapeDtypeStruct((9, 4608), F32),
        ),
        in_specs=[
            pl.BlockSpec(memory_space=pltpu.VMEM),
            pl.BlockSpec(memory_space=pl.ANY),
            pl.BlockSpec(memory_space=pl.ANY),
        ],
        out_specs=(pl.BlockSpec(memory_space=pltpu.VMEM), pl.BlockSpec(memory_space=pltpu.VMEM)),
        scratch_shapes=list(SCRATCH.values()),
        compiler_params=pltpu.CompilerParams(
            collective_id=0, has_side_effects=True, vmem_limit_bytes=62 * 2**20
        ),
    )(clips[0], params, direction)
    return tangent[None], gnv


def solution(mesh):
    in_specs = (P("dp", "frame", None, None), P(), P())
    out_specs = (P("dp", "frame", None, None), P(("dp", "frame"), None))
    return jax.shard_map(body, mesh=mesh, in_specs=in_specs, out_specs=out_specs, check_vma=False)
```

```python
import jax
import jax.numpy as jnp
from jax import lax
from jax.experimental import pallas as pl
from jax.experimental.pallas import tpu as pltpu
from jax.sharding import PartitionSpec as P

MESH = pl.DeviceIdType.MESH
F32 = jnp.float32
BF16 = jnp.bfloat16

D = 1152
HD = 72
HEADS = 8
QKV = 1792
OUT = 640
SCALE = HD ** (-0.5)

S_QKV, S_OUT, T_QKV, T_OUT = 0, 1664, 2304, 3968

HEAD_WINDOWS = [
    (h * HD, (h + 1) * HD, h * HD // 128 * 128, -(-(h + 1) * HD // 128) * 128)
    for h in range(HEADS)
]

LEFTS = ["gy_z", "h2_z", "h2_y", "h2_x", "g_x", "h1_z", "h1_y", "h1_x"]
RIGHTS = {"q1": QKV, "o1": OUT, "q2": QKV, "o2": OUT}

JOBS = [
    (14 * 128, 1024, "zxy", [(0, 512, [("gy_z", "o1", 128)]), (512, 1024, [("h2_z", "q2", 0)])]),
    (22 * 128, 896, "yzx", [(0, 896, [("h2_y", "q2", 512)])]),
    (
        29 * 128,
        896,
        "xyz",
        [
            (0, 256, [("h2_x", "q2", 1408)]),
            (256, 384, [("h2_x", "q2", 1664), ("g_x", "o2", 0)]),
            (384, 896, [("g_x", "o2", 128)]),
        ],
    ),
    (
        10 * 128,
        512,
        "zxy",
        [(0, 384, [("h1_z", "q1", 1280)]), (384, 512, [("h1_z", "q1", 1664), ("gy_z", "o1", 0)])],
    ),
    (5 * 128, 640, "yzx", [(0, 640, [("h1_y", "q1", 640)])]),
    (0, 640, "xyz", [(0, 640, [("h1_x", "q1", 0)])]),
]
N_JOBS = len(JOBS)


def row_moves(order):
    moves = []
    for z in range(4):
        for yh in range(2):
            for c in range(2):
                base = 288 * z + 144 * yh + 72 * c
                if order == "z":
                    moves.append((base, c, 144 * z + 72 * yh, 72))
                    continue
                for x in range(4):
                    if order == "x":
                        moves.append((base + 18 * x, c, 144 * x + 36 * z + 18 * yh, 18))
                        continue
                    for yl in range(2):
                        moves.append((base + 18 * x + 9 * yl, c, 144 * (2 * yh + yl) + 36 * z + 9 * x, 9))
    return moves


def second_rows(axes, second, third):
    if axes == "zxy":
        return 72 * (third // 2) + 18 * second + 9 * (third % 2)
    if axes == "yzx":
        return 36 * second + 9 * third
    return 36 * third + 9 * second


def nn(a, b):
    return jnp.dot(a, b, preferred_element_type=F32)


def nt(a, b):
    return lax.dot_general(a, b, (((1,), (1,)), ((), ())), preferred_element_type=F32)


def tn(a, b):
    return lax.dot_general(a, b, (((0,), (0,)), ((), ())), preferred_element_type=F32)


def left_64(x):
    return pltpu.roll(x, x.shape[1] - 64, 1)


def right_64(x):
    return pltpu.roll(x, 64, 1)


def lane_mask(lo, hi, a, b):
    lane = lax.broadcasted_iota(jnp.int32, (1, b - a), 1) + a
    return (lane >= lo) & (lane < hi)


def add_head(tiles, head, value):
    lo, hi, a, b = HEAD_WINDOWS[head]
    for j in range(a // 128, b // 128):
        piece = value[:, j * 128 - a : (j + 1) * 128 - a]
        mask = lane_mask(lo, hi, j * 128, (j + 1) * 128)
        old = jnp.zeros_like(piece) if tiles[j] is None else tiles[j]
        tiles[j] = jnp.where(mask, piece, old)


def attend(qkv, dqkv, kx, dkx, pn_ref, mask):
    out, tan = [None] * 5, [None] * 5
    for h in range(HEADS):
        lo, hi, a, b = HEAD_WINDOWS[h]
        lanes = jnp.where(lane_mask(lo, hi, a, b), 1.0, 0.0).astype(BF16)
        q = qkv[:, a:b] * lanes
        both = jnp.concatenate([q, dqkv[:, a:b] * lanes], axis=0)
        k, dk = kx[:, a:b], dkx[:, a:b]
        v, dv = qkv[:, 1152 + a : 1152 + b], dqkv[:, 1152 + a : 1152 + b]
        against_k = nt(both, k)
        e = jnp.where(mask, jnp.exp(against_k[:128] * SCALE), 0.0)
        pn = e * (1.0 / jnp.sum(e, axis=1, keepdims=True))
        pn_ref[h] = pn
        p = pn.astype(BF16)
        ds = (against_k[128:] + nt(q, dk)) * SCALE
        dp = (pn * (ds - jnp.sum(pn * ds, axis=1, keepdims=True))).astype(BF16)
        against_v = nn(jnp.concatenate([p, dp], axis=0), v)
        add_head(out, h, against_v[:128])
        add_head(tan, h, against_v[128:] + nn(p, dv))
    return jnp.concatenate(out, axis=1), jnp.concatenate(tan, axis=1)


def attend_back(qkv, kx, pn_ref, go, grad_ref):
    gq, gk, gv = [None] * 5, [None] * 5, [None] * 5
    for h in range(HEADS):
        lo, hi, a, b = HEAD_WINDOWS[h]
        lanes = jnp.where(lane_mask(lo, hi, a, b), 1.0, 0.0).astype(BF16)
        gow = go[:, a:b]
        gp = nt(gow * lanes, qkv[:, 1152 + a : 1152 + b]).astype(BF16).astype(F32)
        pn = pn_ref[h]
        gs = (pn * (gp - jnp.sum(gp * pn, axis=1, keepdims=True)) * SCALE).astype(BF16)
        add_head(gq, h, nn(gs, kx[:, a:b]))
        add_head(gk, h, tn(gs, qkv[:, a:b]))
        add_head(gv, h, tn(pn.astype(BF16), gow))
    gkr = right_64(jnp.concatenate(gk, axis=1))
    for j in range(4):
        grad_ref[:, j * 128 : (j + 1) * 128] = gq[j].astype(BF16)
    grad_ref[:, 512:640] = (gq[4] + gkr[:, :128]).astype(BF16)
    grad_ref[:, 640:1152] = gkr[:, 128:].astype(BF16)
    for j in range(5):
        grad_ref[:, 1152 + j * 128 : 1280 + j * 128] = gv[j].astype(BF16)


def norm_parts(x):
    centred = x - jnp.mean(x, axis=-1, keepdims=True)
    rstd = lax.rsqrt(jnp.mean(centred * centred, axis=-1, keepdims=True) + 1e-06)
    return centred * rstd, rstd


def norm_tangent(normed, rstd, dx):
    return rstd * (
        dx
        - jnp.mean(dx, axis=-1, keepdims=True)
        - normed * jnp.mean(normed * dx, axis=-1, keepdims=True)
    )


def shape_list():
    v = pltpu.VMEM
    dma = pltpu.SemaphoreType.DMA
    scratch = {
        "wp": v((D, 4608), BF16),
        "wd": v((D, 4608), BF16),
        "h1": v((128, D), BF16),
        "qkv1": v((128, QKV), BF16),
        "dqkv1": v((128, QKV), BF16),
        "kx1": v((128, OUT), BF16),
        "dkx": v((128, OUT), BF16),
        "pn1": v((HEADS, 128, 128), F32),
        "qkv2": v((128, QKV), BF16),
        "dqkv2": v((128, QKV), BF16),
        "kx2": v((128, OUT), BF16),
        "pn2": v((HEADS, 128, 128), F32),
        "go": v((128, OUT), BF16),
        "clips_s": v((8, 16, D), BF16),
        "clips_r": v((8, 16, D), BF16),
        "attn_s": v((8, 16, 2 * OUT), BF16),
        "attn_r": v((8, 16, 2 * OUT), BF16),
        "go_s": v((8, 16, OUT), BF16),
        "go_r": v((8, 16, OUT), BF16),
        "tan_s": v((8, 16, D), BF16),
        "tan_r": v((8, 16, D), BF16),
        "lt": v((D, 128), F32),
        "lts": v((2, 576, 128), F32),
        "left": v((len(LEFTS), 576, 256), BF16),
        "left_s": v((len(LEFTS), 576, 128), BF16),
    }
    for name, width in RIGHTS.items():
        scratch["r_" + name] = v((256, width), BF16)
    for i, (_, n, _, _) in enumerate(JOBS):
        scratch[f"p{i}"] = v((4, 144, n), BF16)
        scratch[f"u{i}"] = v((144, n), BF16)
        scratch[f"m{i}"] = v((144, n), BF16)
        scratch[f"v{i}"] = v((2, 144, n), BF16)
        scratch[f"s2_{i}"] = v((4, 48, n), BF16)
        scratch[f"v2_{i}"] = v((3, 48, n), BF16)
        scratch[f"s3_{i}"] = v((4, 16, n), BF16)
        scratch[f"v3_{i}"] = v((3, 16, n), BF16)
    scratch["acc1"] = v((144, 1024), F32)
    scratch["acc2"] = v((48, 1024), F32)
    scratch["pad2"] = v((48, 1024), F32)
    scratch["pad3"] = v((16, 1024), F32)
    scratch["w_sem"] = dma((8,))
    scratch["a_send"] = dma((4, 7))
    scratch["a_recv"] = dma((4, 7))
    scratch["c_send"] = dma((len(LEFTS) + len(RIGHTS),))
    scratch["c_recv"] = dma((len(LEFTS) + len(RIGHTS),))
    scratch["rs_send"] = dma((N_JOBS, 12))
    scratch["rs_recv"] = dma((N_JOBS, 12))
    return scratch


SCRATCH = shape_list()


def kernel(clips_ref, params_ref, direction_ref, tan_ref, gnv_ref, *scratch_refs):
    s = dict(zip(SCRATCH, scratch_refs))
    dp, fr = lax.axis_index("dp"), lax.axis_index("frame")
    core, y_hi, z = dp % 2, dp // 2 % 2, dp // 4
    x, y_lo = fr // 2, fr % 2
    where = {"z": z, "y": 2 * y_hi + y_lo, "x": x}

    def device(at, c):
        return (at["z"] * 4 + at["y"] // 2 * 2 + c, at["x"] * 2 + at["y"] % 2)

    def along(axis, k):
        at = dict(where)
        at[axis] = (at[axis] + k) % 4
        return device(at, core)

    partner = (dp + 1 - 2 * core, fr)

    def remote(src, dst, send, recv, to):
        copy = pltpu.make_async_remote_copy(
            src_ref=src, dst_ref=dst, send_sem=send, recv_sem=recv, device_id=to, device_id_type=MESH
        )
        copy.start()
        sent.append(copy)
        return copy

    sent = []

    loads = []
    for i, (lo, hi) in enumerate([(0, 1792), (1792, 2304), (2304, 4096), (4096, 4608)]):
        pair = []
        for j, (src, dst) in enumerate([(params_ref, s["wp"]), (direction_ref, s["wd"])]):
            copy = pltpu.make_async_copy(src.at[:, lo:hi], dst.at[:, lo:hi], s["w_sem"].at[2 * i + j])
            copy.start()
            pair.append(copy)
        loads.append(pair)

    def loaded(i):
        for copy in loads[i]:
            copy.wait()

    barrier = pltpu.get_barrier_semaphore()
    peers = [along(axis, k) for axis in "zyx" for k in (1, 2, 3)]
    peers += [(dp, (x + k) % 4 * 2 + 1 - y_lo) for k in (1, 2, 3)]
    peers.append(partner)
    for peer in peers:
        pl.semaphore_signal(barrier, inc=1, device_id=peer, device_id_type=MESH)

    natural = clips_ref[...].astype(F32)
    tokens = jnp.concatenate(
        [natural[f, 8 * t : 8 * t + 8] for t in range(8) for f in range(2)], axis=0
    )
    s["clips_s"][...] = tokens.astype(BF16).reshape(8, 16, D)
    h1f, _ = norm_parts(tokens)
    s["h1"][...] = h1f.astype(BF16)

    pl.semaphore_wait(barrier, len(peers))

    def frame_exchange(which, src, dst):
        copies = []
        for k in range(1, 8):
            t = (fr + k) % 8
            copies.append(
                remote(src.at[t], dst.at[fr], s["a_send"].at[which, k - 1], s["a_recv"].at[which, k - 1], (dp, t))
            )
        dst[fr] = src[fr]
        return copies

    def arrived(copies):
        for copy in copies:
            copy.wait_recv()

    clips_copies = frame_exchange(0, s["clips_s"], s["clips_r"])

    left_copies = {}

    def prepare_left(value, names):
        s["lt"][...] = value.T
        for name in names:
            i = LEFTS.index(name)
            for src, c, dst, rows in row_moves(name[-1]):
                s["lts"][c, dst : dst + rows, :] = s["lt"][src : src + rows, :]
            s["left"][i, :, 0:128] = s["lts"][core].astype(BF16)
            s["left_s"][i] = s["lts"][1 - core].astype(BF16)
            left_copies[name] = remote(
                s["left_s"].at[i], s["left"].at[i, :, pl.ds(128, 128)], s["c_send"].at[i], s["c_recv"].at[i], partner
            )

    right_copies = {}

    def share_right(name):
        i = len(LEFTS) + list(RIGHTS).index(name)
        ref = s["r_" + name]
        right_copies[name] = remote(
            ref.at[pl.ds(0, 128)], ref.at[pl.ds(128, 128)], s["c_send"].at[i], s["c_recv"].at[i], partner
        )

    loaded(0)
    for lo in range(0, QKV, 256):
        s["qkv1"][:, lo : lo + 256] = nn(s["h1"][...], s["wp"][:, lo : lo + 256]).astype(BF16)
        s["dqkv1"][:, lo : lo + 256] = nn(s["h1"][...], s["wd"][:, lo : lo + 256]).astype(BF16)

    def align_keys(qkv, kx):
        kx[...] = left_64(qkv[:, 512:1152].astype(F32)).astype(BF16)

    row = lax.broadcasted_iota(jnp.int32, (128, 128), 0)
    col = lax.broadcasted_iota(jnp.int32, (128, 128), 1)
    same_frame = row // 8 % 2 == col // 8 % 2
    same_patch = row % 8 == col % 8
    align_keys(s["qkv1"], s["kx1"])
    align_keys(s["dqkv1"], s["dkx"])
    o1, do1 = attend(s["qkv1"], s["dqkv1"], s["kx1"], s["dkx"], s["pn1"], same_frame)
    s["attn_s"][:, :, 0:OUT] = right_64(o1).astype(BF16).reshape(8, 16, OUT)
    s["attn_s"][:, :, OUT:] = right_64(do1).astype(BF16).reshape(8, 16, OUT)
    attn_copies = frame_exchange(1, s["attn_s"], s["attn_r"])

    prepare_left(h1f.astype(BF16).astype(F32), ["h1_z", "h1_y", "h1_x"])

    arrived(clips_copies)
    loaded(1)
    arrived(attn_copies)
    clips_p = s["clips_r"][...].reshape(128, D).astype(F32)
    o1x = s["attn_r"][:, :, 0:OUT].reshape(128, OUT)
    do1x = s["attn_r"][:, :, OUT:].reshape(128, OUT)
    s["r_o1"][0:128, :] = o1x
    share_right("o1")
    s_out, v_sout = s["wp"][:, S_OUT : S_OUT + OUT], s["wd"][:, S_OUT : S_OUT + OUT]
    through = nt(jnp.concatenate([o1x, do1x], axis=0), s_out)
    y = (clips_p + through[:128]).astype(BF16).astype(F32)
    dy = (through[128:] + nt(o1x, v_sout)).astype(BF16).astype(F32)
    h2f, rstd = norm_parts(y)
    h2 = h2f.astype(BF16)
    h2_both = jnp.concatenate([h2, norm_tangent(h2f, rstd, dy).astype(BF16)], axis=0)
    loaded(2)
    for lo in range(0, QKV, 256):
        wp = s["wp"][:, T_QKV + lo : T_QKV + lo + 256]
        wd = s["wd"][:, T_QKV + lo : T_QKV + lo + 256]
        through = nn(h2_both, wp)
        s["qkv2"][:, lo : lo + 256] = through[:128].astype(BF16)
        s["dqkv2"][:, lo : lo + 256] = (through[128:] + nn(h2, wd)).astype(BF16)
    align_keys(s["qkv2"], s["kx2"])
    align_keys(s["dqkv2"], s["dkx"])
    o2, do2 = attend(s["qkv2"], s["dqkv2"], s["kx2"], s["dkx"], s["pn2"], same_patch)
    o2x, do2x = right_64(o2).astype(BF16), right_64(do2).astype(BF16)
    s["r_o2"][0:128, :] = o2x
    share_right("o2")
    loaded(3)
    t_out, v_tout = s["wp"][:, T_OUT : T_OUT + OUT], s["wd"][:, T_OUT : T_OUT + OUT]
    tangent = (dy + nt(do2x, t_out) + nt(o2x, v_tout)).astype(BF16)
    s["tan_s"][...] = tangent.reshape(8, 16, D)
    tan_copies = frame_exchange(3, s["tan_s"], s["tan_r"])
    g = (tangent.astype(F32) * (16384 ** (-0.5))).astype(BF16)
    s["go"][...] = left_64(nn(g, t_out)).astype(BF16)
    attend_back(s["qkv2"], s["kx2"], s["pn2"], s["go"], s["r_q2"].at[pl.ds(0, 128)])
    share_right("q2")
    gq2 = s["r_q2"][0:128, :]
    gh2 = nt(gq2, s["wp"][:, T_QKV : T_QKV + QKV])
    gy = (g.astype(F32) + norm_tangent(h2f, rstd, gh2)).astype(BF16)
    s["go_s"][...] = nn(gy, s_out).astype(BF16).reshape(8, 16, OUT)
    go_copies = frame_exchange(2, s["go_s"], s["go_r"])

    s["pad2"][...] = jnp.zeros_like(s["pad2"])
    s["pad3"][...] = jnp.zeros_like(s["pad3"])
    flight = {}

    def product(job):
        _, n, axes, segments = JOBS[job]
        needed = [name for _, _, terms in segments for left, right, _ in terms for name in (left, right)]
        for name in needed:
            copies = left_copies if name in left_copies else right_copies
            if name not in shared:
                copies[name].wait_recv()
                shared.append(name)
        part, first_in, ready = s[f"p{job}"], s[f"u{job}"], s[f"v{job}"]
        for lo, hi, terms in segments:
            acc = None
            for left, right, at in terms:
                term = nn(s["left"][LEFTS.index(left)], s["r_" + right][:, at : at + hi - lo])
                acc = term if acc is None else acc + term
            part[:, :, lo:hi] = acc.astype(BF16).reshape(4, 144, hi - lo)
        here = where[axes[0]]
        right, left = along(axes[0], 1), along(axes[0], 3)
        ahead, behind, across = (here + 1) % 4, (here + 3) % 4, (here + 2) % 4
        flight[job] = [
            remote(src.at[pl.ds(at, rows)], dst.at[pl.ds(at, rows)], s["rs_send"].at[job, i], s["rs_recv"].at[job, i], to)
            for i, (src, dst, at, rows, to) in enumerate(
                [
                    (part.at[across], first_in, 0, 80, right),
                    (part.at[across], first_in, 80, 64, left),
                    (part.at[ahead], ready.at[0], 80, 64, right),
                    (part.at[behind], ready.at[1], 0, 80, left),
                ]
            )
        ]

    def merge(job):
        here = where[JOBS[job][2][0]]
        part, first_in, merged, ready = s[f"p{job}"], s[f"u{job}"], s[f"m{job}"], s[f"v{job}"]
        for i, k, at, rows in [(0, 1, 0, 80), (1, 3, 80, 64)]:
            flight[job][i].wait_recv()
            own = part[(here + k) % 4, at : at + rows].astype(F32)
            merged[at : at + rows] = (own + first_in[at : at + rows].astype(F32)).astype(BF16)
            flight[job].append(
                remote(
                    merged.at[pl.ds(at, rows)],
                    ready.at[i, pl.ds(at, rows)],
                    s["rs_send"].at[job, 4 + i],
                    s["rs_recv"].at[job, 4 + i],
                    along(JOBS[job][2][0], k),
                )
            )

    def scatter(job, stage, src, dst):
        axis = JOBS[job][2][stage]
        flight[job] = []
        for k in (1, 2, 3):
            i = 3 + 3 * stage + k - 1
            flight[job].append(
                remote(
                    src.at[(where[axis] + k) % 4],
                    dst.at[k - 1],
                    s["rs_send"].at[job, i],
                    s["rs_recv"].at[job, i],
                    along(axis, k),
                )
            )

    def second_stage(job):
        _, n, axes, _ = JOBS[job]
        arrived(flight[job][2:])
        part, ready = s[f"p{job}"], s[f"v{job}"]
        s["acc1"][:, :n] = part[where[axes[0]]].astype(F32) + ready[0].astype(F32) + ready[1].astype(F32)
        for second in range(4):
            for third in range(4):
                at = second_rows(axes, second, third)
                s["pad2"][9 * third : 9 * third + 9, :n] = s["acc1"][at : at + 9, :n]
            s[f"s2_{job}"][second] = s["pad2"][:, :n].astype(BF16)
        scatter(job, 1, s[f"s2_{job}"], s[f"v2_{job}"])

    def total(job, stage, src, dst):
        arrived(flight[job])
        mine = src[where[JOBS[job][2][stage]]].astype(F32)
        return mine + dst[0].astype(F32) + dst[1].astype(F32) + dst[2].astype(F32)

    def third_stage(job):
        n = JOBS[job][1]
        s["acc2"][:, :n] = total(job, 1, s[f"s2_{job}"], s[f"v2_{job}"])
        for third in range(4):
            s["pad3"][0:9, :n] = s["acc2"][9 * third : 9 * third + 9, :n]
            s[f"s3_{job}"][third] = s["pad3"][:, :n].astype(BF16)
        scatter(job, 2, s[f"s3_{job}"], s[f"v3_{job}"])

    def finish(job):
        first, n, _, _ = JOBS[job]
        gnv_ref[:, first : first + n] = total(job, 2, s[f"s3_{job}"], s[f"v3_{job}"])[0:9]

    shared = []
    prepare_left(h2.astype(F32), ["h2_y", "h2_x"])
    prepare_left(g.astype(F32), ["g_x"])
    product(1)
    product(2)

    arrived(go_copies)
    s["go"][...] = left_64(s["go_r"][...].reshape(128, OUT).astype(F32)).astype(BF16)
    attend_back(s["qkv1"], s["kx1"], s["pn1"], s["go"], s["r_q1"].at[pl.ds(0, 128)])
    share_right("q1")

    merge(1)
    merge(2)
    prepare_left(gy.astype(F32), ["gy_z"])
    prepare_left(h2.astype(F32), ["h2_z"])
    product(0)
    product(4)
    product(5)
    product(3)
    arrived(tan_copies)
    tan = s["tan_r"][...].reshape(128, D).astype(F32)
    for f in range(2):
        tan_ref[f] = jnp.concatenate(
            [tan[16 * t + 8 * f : 16 * t + 8 * f + 8] for t in range(8)], axis=0
        ).astype(BF16)
    merge(0)
    second_stage(1)
    second_stage(2)
    merge(4)
    merge(5)
    merge(3)
    second_stage(0)
    third_stage(1)
    third_stage(2)
    second_stage(4)
    second_stage(5)
    second_stage(3)
    third_stage(0)
    finish(1)
    finish(2)
    third_stage(4)
    third_stage(5)
    third_stage(3)
    finish(0)
    finish(4)
    finish(5)
    finish(3)

    for copy in sent:
        copy.wait_send()


def place(tan_in, gnv_in, tan_out, gnv_out, sem):
    copies = [
        pltpu.make_async_copy(tan_in, tan_out, sem.at[0]),
        pltpu.make_async_copy(gnv_in, gnv_out, sem.at[1]),
    ]
    for copy in copies:
        copy.start()
    for copy in copies:
        copy.wait()


def body(clips, params, direction):
    tangent, gnv = pl.pallas_call(
        kernel,
        out_shape=(
            jax.ShapeDtypeStruct((2, 64, D), BF16),
            jax.ShapeDtypeStruct((9, 4608), F32),
        ),
        in_specs=[
            pl.BlockSpec(memory_space=pltpu.VMEM),
            pl.BlockSpec(memory_space=pl.ANY),
            pl.BlockSpec(memory_space=pl.ANY),
        ],
        out_specs=(pl.BlockSpec(memory_space=pltpu.VMEM), pl.BlockSpec(memory_space=pltpu.VMEM)),
        scratch_shapes=list(SCRATCH.values()),
        compiler_params=pltpu.CompilerParams(
            collective_id=0, has_side_effects=True, vmem_limit_bytes=62 * 2**20
        ),
    )(clips[0], params, direction)
    tangent, gnv = pl.pallas_call(
        place,
        out_shape=(
            jax.ShapeDtypeStruct((2, 64, D), BF16),
            jax.ShapeDtypeStruct((9, 4608), F32),
        ),
        in_specs=[pl.BlockSpec(memory_space=pl.ANY)] * 2,
        out_specs=(pl.BlockSpec(memory_space=pl.ANY),) * 2,
        scratch_shapes=[pltpu.SemaphoreType.DMA((2,))],
    )(tangent, gnv)
    return tangent[None], gnv


def solution(mesh):
    in_specs = (P("dp", "frame", None, None), P(), P())
    out_specs = (P("dp", "frame", None, None), P(("dp", "frame"), None))
    return jax.shard_map(body, mesh=mesh, in_specs=in_specs, out_specs=out_specs, check_vma=False)
```

```python
import jax
import jax.numpy as jnp
from jax import lax
from jax.experimental import pallas as pl
from jax.experimental.pallas import tpu as pltpu
from jax.sharding import PartitionSpec as P

MESH = pl.DeviceIdType.MESH
F32 = jnp.float32
BF16 = jnp.bfloat16

D = 1152
HD = 72
HEADS = 8
QKV = 1792
OUT = 640
SCALE = HD ** (-0.5)

S_QKV, S_OUT, T_QKV, T_OUT = 0, 1664, 2304, 3968

HEAD_WINDOWS = [
    (h * HD, (h + 1) * HD, h * HD // 128 * 128, -(-(h + 1) * HD // 128) * 128)
    for h in range(HEADS)
]

LEFTS = ["gy_z", "h2_z", "h2_y", "h2_x", "g_x", "h1_z", "h1_y", "h1_x"]
RIGHTS = {"q1": QKV, "o1": OUT, "q2": QKV, "o2": OUT}

JOBS = [
    (14 * 128, 1024, "zxy", [(0, 512, [("gy_z", "o1", 128)]), (512, 1024, [("h2_z", "q2", 0)])]),
    (22 * 128, 896, "yzx", [(0, 896, [("h2_y", "q2", 512)])]),
    (
        29 * 128,
        896,
        "xyz",
        [
            (0, 256, [("h2_x", "q2", 1408)]),
            (256, 384, [("h2_x", "q2", 1664), ("g_x", "o2", 0)]),
            (384, 896, [("g_x", "o2", 128)]),
        ],
    ),
    (
        10 * 128,
        512,
        "zxy",
        [(0, 384, [("h1_z", "q1", 1280)]), (384, 512, [("h1_z", "q1", 1664), ("gy_z", "o1", 0)])],
    ),
    (5 * 128, 640, "yzx", [(0, 640, [("h1_y", "q1", 640)])]),
    (0, 640, "xyz", [(0, 640, [("h1_x", "q1", 0)])]),
]
N_JOBS = len(JOBS)


def row_moves(order):
    moves = []
    for z in range(4):
        for yh in range(2):
            for c in range(2):
                base = 288 * z + 144 * yh + 72 * c
                if order == "z":
                    moves.append((base, c, 144 * z + 72 * yh, 72))
                    continue
                for x in range(4):
                    if order == "x":
                        moves.append((base + 18 * x, c, 144 * x + 36 * z + 18 * yh, 18))
                        continue
                    for yl in range(2):
                        moves.append((base + 18 * x + 9 * yl, c, 144 * (2 * yh + yl) + 36 * z + 9 * x, 9))
    return moves


def second_rows(axes, second, third):
    if axes == "zxy":
        return 72 * (third // 2) + 18 * second + 9 * (third % 2)
    if axes == "yzx":
        return 36 * second + 9 * third
    return 36 * third + 9 * second


def nn(a, b):
    return jnp.dot(a, b, preferred_element_type=F32)


def nt(a, b):
    return lax.dot_general(a, b, (((1,), (1,)), ((), ())), preferred_element_type=F32)


def tn(a, b):
    return lax.dot_general(a, b, (((0,), (0,)), ((), ())), preferred_element_type=F32)


def left_64(x):
    return pltpu.roll(x, x.shape[1] - 64, 1)


def right_64(x):
    return pltpu.roll(x, 64, 1)


def lane_mask(lo, hi, a, b):
    lane = lax.broadcasted_iota(jnp.int32, (1, b - a), 1) + a
    return (lane >= lo) & (lane < hi)


def add_head(tiles, head, value):
    lo, hi, a, b = HEAD_WINDOWS[head]
    for j in range(a // 128, b // 128):
        piece = value[:, j * 128 - a : (j + 1) * 128 - a]
        mask = lane_mask(lo, hi, j * 128, (j + 1) * 128)
        old = jnp.zeros_like(piece) if tiles[j] is None else tiles[j]
        tiles[j] = jnp.where(mask, piece, old)


def first_part(tiles):
    moved = right_64(jnp.concatenate(tiles[:3], axis=1))
    return jnp.where(lane_mask(64, 384, 0, 384), moved, 0.0).astype(BF16)


def second_part(tiles):
    return left_64(jnp.concatenate(tiles[2:], axis=1))[:, :256].astype(BF16)


def attend(qkv, dqkv, kx, dkx, pn_ref, mask, after_head_4):
    out, tan = [None] * 5, [None] * 5
    for h in range(HEADS):
        lo, hi, a, b = HEAD_WINDOWS[h]
        lanes = jnp.where(lane_mask(lo, hi, a, b), 1.0, 0.0).astype(BF16)
        q = qkv[:, a:b] * lanes
        both = jnp.concatenate([q, dqkv[:, a:b] * lanes], axis=0)
        k, dk = kx[:, a:b], dkx[:, a:b]
        v, dv = qkv[:, 1152 + a : 1152 + b], dqkv[:, 1152 + a : 1152 + b]
        against_k = nt(both, k)
        e = jnp.where(mask, jnp.exp(against_k[:128] * SCALE), 0.0)
        pn = e * (1.0 / jnp.sum(e, axis=1, keepdims=True))
        pn_ref[h] = pn
        p = pn.astype(BF16)
        ds = (against_k[128:] + nt(q, dk)) * SCALE
        dp = (pn * (ds - jnp.sum(pn * ds, axis=1, keepdims=True))).astype(BF16)
        against_v = nn(jnp.concatenate([p, dp], axis=0), v)
        add_head(out, h, against_v[:128])
        add_head(tan, h, against_v[128:] + nn(p, dv))
        if h == 4:
            after_head_4(out, tan)
    return out, tan


def attend_back(qkv, kx, pn_ref, go, grad_ref):
    gq, gk, gv = [None] * 5, [None] * 5, [None] * 5
    for h in range(HEADS):
        lo, hi, a, b = HEAD_WINDOWS[h]
        lanes = jnp.where(lane_mask(lo, hi, a, b), 1.0, 0.0).astype(BF16)
        gow = go[:, a:b]
        gp = nt(gow * lanes, qkv[:, 1152 + a : 1152 + b]).astype(BF16).astype(F32)
        pn = pn_ref[h]
        gs = (pn * (gp - jnp.sum(gp * pn, axis=1, keepdims=True)) * SCALE).astype(BF16)
        add_head(gq, h, nn(gs, kx[:, a:b]))
        add_head(gk, h, tn(gs, qkv[:, a:b]))
        add_head(gv, h, tn(pn.astype(BF16), gow))
    gkr = right_64(jnp.concatenate(gk, axis=1))
    for j in range(4):
        grad_ref[:, j * 128 : (j + 1) * 128] = gq[j].astype(BF16)
    grad_ref[:, 512:640] = (gq[4] + gkr[:, :128]).astype(BF16)
    grad_ref[:, 640:1152] = gkr[:, 128:].astype(BF16)
    for j in range(5):
        grad_ref[:, 1152 + j * 128 : 1280 + j * 128] = gv[j].astype(BF16)


def norm_parts(x):
    centred = x - jnp.mean(x, axis=-1, keepdims=True)
    rstd = lax.rsqrt(jnp.mean(centred * centred, axis=-1, keepdims=True) + 1e-06)
    return centred * rstd, rstd


def norm_tangent(normed, rstd, dx):
    return rstd * (
        dx
        - jnp.mean(dx, axis=-1, keepdims=True)
        - normed * jnp.mean(normed * dx, axis=-1, keepdims=True)
    )


def shape_list():
    v = pltpu.VMEM
    dma = pltpu.SemaphoreType.DMA
    scratch = {
        "wp": v((D, 4608), BF16),
        "wd": v((D, 4608), BF16),
        "h1": v((128, D), BF16),
        "qkv1": v((128, QKV), BF16),
        "dqkv1": v((128, QKV), BF16),
        "kx1": v((128, OUT), BF16),
        "dkx": v((128, OUT), BF16),
        "pn1": v((HEADS, 128, 128), F32),
        "qkv2": v((128, QKV), BF16),
        "dqkv2": v((128, QKV), BF16),
        "kx2": v((128, OUT), BF16),
        "pn2": v((HEADS, 128, 128), F32),
        "go": v((128, OUT), BF16),
        "clips_s": v((8, 16, D), BF16),
        "clips_r": v((8, 16, D), BF16),
        "attn_s": v((8, 16, 768), BF16),
        "attn_r": v((8, 16, 768), BF16),
        "attn2_s": v((8, 16, 512), BF16),
        "attn2_r": v((8, 16, 512), BF16),
        "go_s": v((8, 16, OUT), BF16),
        "go_r": v((8, 16, OUT), BF16),
        "tan_s": v((8, 16, D), BF16),
        "tan_r": v((8, 16, D), BF16),
        "lt": v((D, 128), F32),
        "lts": v((2, 576, 128), F32),
        "left": v((len(LEFTS), 576, 256), BF16),
        "left_s": v((len(LEFTS), 576, 128), BF16),
    }
    for name, width in RIGHTS.items():
        scratch["r_" + name] = v((256, width), BF16)
    for i, (_, n, _, _) in enumerate(JOBS):
        scratch[f"p{i}"] = v((4, 144, n), BF16)
        scratch[f"u{i}"] = v((144, n), BF16)
        scratch[f"m{i}"] = v((144, n), BF16)
        scratch[f"v{i}"] = v((2, 144, n), BF16)
        scratch[f"s2_{i}"] = v((4, 48, n), BF16)
        scratch[f"v2_{i}"] = v((3, 48, n), BF16)
        scratch[f"s3_{i}"] = v((4, 16, n), BF16)
        scratch[f"v3_{i}"] = v((3, 16, n), BF16)
    scratch["acc1"] = v((144, 1024), F32)
    scratch["acc2"] = v((48, 1024), F32)
    scratch["pad2"] = v((48, 1024), F32)
    scratch["pad3"] = v((16, 1024), F32)
    scratch["w_sem"] = dma((8,))
    scratch["a_send"] = dma((5, 7))
    scratch["a_recv"] = dma((5, 7))
    scratch["c_send"] = dma((len(LEFTS) + len(RIGHTS),))
    scratch["c_recv"] = dma((len(LEFTS) + len(RIGHTS),))
    scratch["rs_send"] = dma((N_JOBS, 12))
    scratch["rs_recv"] = dma((N_JOBS, 12))
    return scratch


SCRATCH = shape_list()


def kernel(clips_ref, params_ref, direction_ref, tan_ref, gnv_ref, *scratch_refs):
    s = dict(zip(SCRATCH, scratch_refs))
    dp, fr = lax.axis_index("dp"), lax.axis_index("frame")
    core, y_hi, z = dp % 2, dp // 2 % 2, dp // 4
    x, y_lo = fr // 2, fr % 2
    where = {"z": z, "y": 2 * y_hi + y_lo, "x": x}

    def device(at, c):
        return (at["z"] * 4 + at["y"] // 2 * 2 + c, at["x"] * 2 + at["y"] % 2)

    def along(axis, k):
        at = dict(where)
        at[axis] = (at[axis] + k) % 4
        return device(at, core)

    partner = (dp + 1 - 2 * core, fr)

    def remote(src, dst, send, recv, to):
        copy = pltpu.make_async_remote_copy(
            src_ref=src, dst_ref=dst, send_sem=send, recv_sem=recv, device_id=to, device_id_type=MESH
        )
        copy.start()
        sent.append(copy)
        return copy

    sent = []

    loads = []
    for i, (lo, hi) in enumerate([(0, 1792), (1792, 2304), (2304, 4096), (4096, 4608)]):
        pair = []
        for j, (src, dst) in enumerate([(params_ref, s["wp"]), (direction_ref, s["wd"])]):
            copy = pltpu.make_async_copy(src.at[:, lo:hi], dst.at[:, lo:hi], s["w_sem"].at[2 * i + j])
            copy.start()
            pair.append(copy)
        loads.append(pair)

    def loaded(i):
        for copy in loads[i]:
            copy.wait()

    barrier = pltpu.get_barrier_semaphore()
    peers = [along(axis, k) for axis in "zyx" for k in (1, 2, 3)]
    peers += [(dp, (x + k) % 4 * 2 + 1 - y_lo) for k in (1, 2, 3)]
    peers.append(partner)
    for peer in peers:
        pl.semaphore_signal(barrier, inc=1, device_id=peer, device_id_type=MESH)

    natural = clips_ref[...].astype(F32)
    tokens = jnp.concatenate(
        [natural[f, 8 * t : 8 * t + 8] for t in range(8) for f in range(2)], axis=0
    )
    s["clips_s"][...] = tokens.astype(BF16).reshape(8, 16, D)
    h1f, _ = norm_parts(tokens)
    s["h1"][...] = h1f.astype(BF16)

    pl.semaphore_wait(barrier, len(peers))

    def frame_exchange(which, src, dst):
        copies = []
        for k in range(1, 8):
            t = (fr + k) % 8
            copies.append(
                remote(src.at[t], dst.at[fr], s["a_send"].at[which, k - 1], s["a_recv"].at[which, k - 1], (dp, t))
            )
        dst[fr] = src[fr]
        return copies

    def arrived(copies):
        for copy in copies:
            copy.wait_recv()

    clips_copies = frame_exchange(0, s["clips_s"], s["clips_r"])

    left_copies = {}

    def prepare_left(value, names):
        s["lt"][...] = value.T
        for name in names:
            i = LEFTS.index(name)
            for src, c, dst, rows in row_moves(name[-1]):
                s["lts"][c, dst : dst + rows, :] = s["lt"][src : src + rows, :]
            s["left"][i, :, 0:128] = s["lts"][core].astype(BF16)
            s["left_s"][i] = s["lts"][1 - core].astype(BF16)
            left_copies[name] = remote(
                s["left_s"].at[i], s["left"].at[i, :, pl.ds(128, 128)], s["c_send"].at[i], s["c_recv"].at[i], partner
            )

    right_copies = {}

    def share_right(name):
        i = len(LEFTS) + list(RIGHTS).index(name)
        ref = s["r_" + name]
        right_copies[name] = remote(
            ref.at[pl.ds(0, 128)], ref.at[pl.ds(128, 128)], s["c_send"].at[i], s["c_recv"].at[i], partner
        )

    loaded(0)
    for lo in range(0, QKV, 256):
        s["qkv1"][:, lo : lo + 256] = nn(s["h1"][...], s["wp"][:, lo : lo + 256]).astype(BF16)
        s["dqkv1"][:, lo : lo + 256] = nn(s["h1"][...], s["wd"][:, lo : lo + 256]).astype(BF16)

    def align_keys(qkv, kx):
        kx[...] = left_64(qkv[:, 512:1152].astype(F32)).astype(BF16)

    row = lax.broadcasted_iota(jnp.int32, (128, 128), 0)
    col = lax.broadcasted_iota(jnp.int32, (128, 128), 1)
    same_frame = row // 8 % 2 == col // 8 % 2
    same_patch = row % 8 == col % 8
    align_keys(s["qkv1"], s["kx1"])
    align_keys(s["dqkv1"], s["dkx"])
    attn_copies = []

    def send_first(out, tan):
        s["attn_s"][:, :, 0:384] = first_part(out).reshape(8, 16, 384)
        s["attn_s"][:, :, 384:768] = first_part(tan).reshape(8, 16, 384)
        attn_copies.extend(frame_exchange(1, s["attn_s"], s["attn_r"]))

    o1, do1 = attend(s["qkv1"], s["dqkv1"], s["kx1"], s["dkx"], s["pn1"], same_frame, send_first)
    s["attn2_s"][:, :, 0:256] = second_part(o1).reshape(8, 16, 256)
    s["attn2_s"][:, :, 256:512] = second_part(do1).reshape(8, 16, 256)
    attn_copies.extend(frame_exchange(4, s["attn2_s"], s["attn2_r"]))

    prepare_left(h1f.astype(BF16).astype(F32), ["h1_z", "h1_y", "h1_x"])

    arrived(clips_copies)
    loaded(1)
    arrived(attn_copies)
    clips_p = s["clips_r"][...].reshape(128, D).astype(F32)
    parts = s["attn_r"][...].reshape(128, 768), s["attn2_r"][...].reshape(128, 512)
    o1x = jnp.concatenate([parts[0][:, :384], parts[1][:, :256]], axis=1)
    do1x = jnp.concatenate([parts[0][:, 384:], parts[1][:, 256:]], axis=1)
    s["r_o1"][0:128, :] = o1x
    share_right("o1")
    s_out, v_sout = s["wp"][:, S_OUT : S_OUT + OUT], s["wd"][:, S_OUT : S_OUT + OUT]
    through = nt(jnp.concatenate([o1x, do1x], axis=0), s_out)
    y = (clips_p + through[:128]).astype(BF16).astype(F32)
    dy = (through[128:] + nt(o1x, v_sout)).astype(BF16).astype(F32)
    h2f, rstd = norm_parts(y)
    h2 = h2f.astype(BF16)
    h2_both = jnp.concatenate([h2, norm_tangent(h2f, rstd, dy).astype(BF16)], axis=0)
    loaded(2)
    for lo in range(0, QKV, 256):
        wp = s["wp"][:, T_QKV + lo : T_QKV + lo + 256]
        wd = s["wd"][:, T_QKV + lo : T_QKV + lo + 256]
        through = nn(h2_both, wp)
        s["qkv2"][:, lo : lo + 256] = through[:128].astype(BF16)
        s["dqkv2"][:, lo : lo + 256] = (through[128:] + nn(h2, wd)).astype(BF16)
    align_keys(s["qkv2"], s["kx2"])
    align_keys(s["dqkv2"], s["dkx"])
    o2, do2 = attend(s["qkv2"], s["dqkv2"], s["kx2"], s["dkx"], s["pn2"], same_patch, lambda *_: None)
    o2x = right_64(jnp.concatenate(o2, axis=1)).astype(BF16)
    do2x = right_64(jnp.concatenate(do2, axis=1)).astype(BF16)
    s["r_o2"][0:128, :] = o2x
    share_right("o2")
    loaded(3)
    t_out, v_tout = s["wp"][:, T_OUT : T_OUT + OUT], s["wd"][:, T_OUT : T_OUT + OUT]
    tangent = (dy + nt(do2x, t_out) + nt(o2x, v_tout)).astype(BF16)
    s["tan_s"][...] = tangent.reshape(8, 16, D)
    tan_copies = frame_exchange(3, s["tan_s"], s["tan_r"])
    g = (tangent.astype(F32) * (16384 ** (-0.5))).astype(BF16)
    s["go"][...] = left_64(nn(g, t_out)).astype(BF16)
    attend_back(s["qkv2"], s["kx2"], s["pn2"], s["go"], s["r_q2"].at[pl.ds(0, 128)])
    share_right("q2")
    gq2 = s["r_q2"][0:128, :]
    gh2 = nt(gq2, s["wp"][:, T_QKV : T_QKV + QKV])
    gy = (g.astype(F32) + norm_tangent(h2f, rstd, gh2)).astype(BF16)
    s["go_s"][...] = nn(gy, s_out).astype(BF16).reshape(8, 16, OUT)
    go_copies = frame_exchange(2, s["go_s"], s["go_r"])

    s["pad2"][...] = jnp.zeros_like(s["pad2"])
    s["pad3"][...] = jnp.zeros_like(s["pad3"])
    flight = {}

    def product(job):
        _, n, axes, segments = JOBS[job]
        needed = [name for _, _, terms in segments for left, right, _ in terms for name in (left, right)]
        for name in needed:
            copies = left_copies if name in left_copies else right_copies
            if name not in shared:
                copies[name].wait_recv()
                shared.append(name)
        part, first_in, ready = s[f"p{job}"], s[f"u{job}"], s[f"v{job}"]
        for lo, hi, terms in segments:
            acc = None
            for left, right, at in terms:
                term = nn(s["left"][LEFTS.index(left)], s["r_" + right][:, at : at + hi - lo])
                acc = term if acc is None else acc + term
            part[:, :, lo:hi] = acc.astype(BF16).reshape(4, 144, hi - lo)
        here = where[axes[0]]
        right, left = along(axes[0], 1), along(axes[0], 3)
        ahead, behind, across = (here + 1) % 4, (here + 3) % 4, (here + 2) % 4
        flight[job] = [
            remote(src.at[pl.ds(at, rows)], dst.at[pl.ds(at, rows)], s["rs_send"].at[job, i], s["rs_recv"].at[job, i], to)
            for i, (src, dst, at, rows, to) in enumerate(
                [
                    (part.at[across], first_in, 0, 80, right),
                    (part.at[across], first_in, 80, 64, left),
                    (part.at[ahead], ready.at[0], 80, 64, right),
                    (part.at[behind], ready.at[1], 0, 80, left),
                ]
            )
        ]

    def merge(job):
        here = where[JOBS[job][2][0]]
        part, first_in, merged, ready = s[f"p{job}"], s[f"u{job}"], s[f"m{job}"], s[f"v{job}"]
        for i, k, at, rows in [(0, 1, 0, 80), (1, 3, 80, 64)]:
            flight[job][i].wait_recv()
            own = part[(here + k) % 4, at : at + rows].astype(F32)
            merged[at : at + rows] = (own + first_in[at : at + rows].astype(F32)).astype(BF16)
            flight[job].append(
                remote(
                    merged.at[pl.ds(at, rows)],
                    ready.at[i, pl.ds(at, rows)],
                    s["rs_send"].at[job, 4 + i],
                    s["rs_recv"].at[job, 4 + i],
                    along(JOBS[job][2][0], k),
                )
            )

    def scatter(job, stage, src, dst):
        axis = JOBS[job][2][stage]
        flight[job] = []
        for k in (1, 2, 3):
            i = 3 + 3 * stage + k - 1
            flight[job].append(
                remote(
                    src.at[(where[axis] + k) % 4],
                    dst.at[k - 1],
                    s["rs_send"].at[job, i],
                    s["rs_recv"].at[job, i],
                    along(axis, k),
                )
            )

    def second_stage(job):
        _, n, axes, _ = JOBS[job]
        arrived(flight[job][2:])
        part, ready = s[f"p{job}"], s[f"v{job}"]
        s["acc1"][:, :n] = part[where[axes[0]]].astype(F32) + ready[0].astype(F32) + ready[1].astype(F32)
        for second in range(4):
            for third in range(4):
                at = second_rows(axes, second, third)
                s["pad2"][9 * third : 9 * third + 9, :n] = s["acc1"][at : at + 9, :n]
            s[f"s2_{job}"][second] = s["pad2"][:, :n].astype(BF16)
        scatter(job, 1, s[f"s2_{job}"], s[f"v2_{job}"])

    def total(job, stage, src, dst):
        arrived(flight[job])
        mine = src[where[JOBS[job][2][stage]]].astype(F32)
        return mine + dst[0].astype(F32) + dst[1].astype(F32) + dst[2].astype(F32)

    def third_stage(job):
        n = JOBS[job][1]
        s["acc2"][:, :n] = total(job, 1, s[f"s2_{job}"], s[f"v2_{job}"])
        for third in range(4):
            s["pad3"][0:9, :n] = s["acc2"][9 * third : 9 * third + 9, :n]
            s[f"s3_{job}"][third] = s["pad3"][:, :n].astype(BF16)
        scatter(job, 2, s[f"s3_{job}"], s[f"v3_{job}"])

    def finish(job):
        first, n, _, _ = JOBS[job]
        gnv_ref[:, first : first + n] = total(job, 2, s[f"s3_{job}"], s[f"v3_{job}"])[0:9]

    shared = []
    prepare_left(gy.astype(F32), ["gy_z"])
    prepare_left(h2.astype(F32), ["h2_y", "h2_x", "h2_z"])
    prepare_left(g.astype(F32), ["g_x"])
    product(1)
    product(2)
    product(0)

    arrived(go_copies)
    s["go"][...] = left_64(s["go_r"][...].reshape(128, OUT).astype(F32)).astype(BF16)
    attend_back(s["qkv1"], s["kx1"], s["pn1"], s["go"], s["r_q1"].at[pl.ds(0, 128)])
    share_right("q1")

    merge(1)
    merge(2)
    merge(0)
    product(4)
    product(5)
    product(3)
    arrived(tan_copies)
    tan = s["tan_r"][...].reshape(128, D).astype(F32)
    for f in range(2):
        tan_ref[f] = jnp.concatenate(
            [tan[16 * t + 8 * f : 16 * t + 8 * f + 8] for t in range(8)], axis=0
        ).astype(BF16)
    second_stage(1)
    second_stage(2)
    second_stage(0)
    merge(4)
    merge(5)
    merge(3)
    third_stage(1)
    third_stage(2)
    third_stage(0)
    second_stage(4)
    second_stage(5)
    second_stage(3)
    finish(1)
    finish(2)
    finish(0)
    third_stage(4)
    third_stage(5)
    third_stage(3)
    finish(4)
    finish(5)
    finish(3)

    for copy in sent:
        copy.wait_send()


def place(tan_in, gnv_in, tan_out, gnv_out):
    tan_out[...] = tan_in[...]
    gnv_out[...] = gnv_in[...]


def body(clips, params, direction):
    tangent, gnv = pl.pallas_call(
        kernel,
        out_shape=(
            jax.ShapeDtypeStruct((2, 64, D), BF16),
            jax.ShapeDtypeStruct((9, 4608), F32),
        ),
        in_specs=[
            pl.BlockSpec(memory_space=pltpu.VMEM),
            pl.BlockSpec(memory_space=pl.ANY),
            pl.BlockSpec(memory_space=pl.ANY),
        ],
        out_specs=(pl.BlockSpec(memory_space=pltpu.VMEM), pl.BlockSpec(memory_space=pltpu.VMEM)),
        scratch_shapes=list(SCRATCH.values()),
        compiler_params=pltpu.CompilerParams(
            collective_id=0, has_side_effects=True, vmem_limit_bytes=62 * 2**20
        ),
    )(clips[0], params, direction)
    tangent, gnv = pl.pallas_call(
        place,
        out_shape=(
            jax.ShapeDtypeStruct((2, 64, D), BF16),
            jax.ShapeDtypeStruct((9, 4608), F32),
        ),
        in_specs=[pl.BlockSpec(memory_space=pltpu.VMEM)] * 2,
        out_specs=(pl.BlockSpec(memory_space=pltpu.VMEM),) * 2,
    )(tangent, gnv)
    return tangent[None], gnv


def solution(mesh):
    in_specs = (P("dp", "frame", None, None), P(), P())
    out_specs = (P("dp", "frame", None, None), P(("dp", "frame"), None))
    return jax.shard_map(body, mesh=mesh, in_specs=in_specs, out_specs=out_specs, check_vma=False)
```

```python
import jax
import jax.numpy as jnp
from jax import lax
from jax.experimental import pallas as pl
from jax.experimental.pallas import tpu as pltpu
from jax.sharding import PartitionSpec as P

MESH = pl.DeviceIdType.MESH
F32 = jnp.float32
BF16 = jnp.bfloat16

D = 1152
HD = 72
HEADS = 8
QKV = 1792
OUT = 640
SCALE = HD ** (-0.5)

S_QKV, S_OUT, T_QKV, T_OUT = 0, 1664, 2304, 3968

HEAD_WINDOWS = [
    (h * HD, (h + 1) * HD, h * HD // 128 * 128, -(-(h + 1) * HD // 128) * 128)
    for h in range(HEADS)
]

LEFTS = ["g_z", "g_x", "h2_y", "h2_x", "gy_z", "h1_z", "h1_y", "h1_x"]
RIGHTS = {"q1": QKV, "o1": OUT, "q2": QKV, "o2": OUT}

JOBS = [
    (32 * 128, 512, "zxy", [(0, 512, [("g_z", "o2", 128)])]),
    (18 * 128, 896, "yzx", [(0, 896, [("h2_y", "q2", 0)])]),
    (
        25 * 128,
        896,
        "xyz",
        [(0, 768, [("h2_x", "q2", 896)]), (768, 896, [("h2_x", "q2", 1664), ("g_x", "o2", 0)])],
    ),
    (14 * 128, 512, "zxy", [(0, 512, [("gy_z", "o1", 128)])]),
    (
        10 * 128,
        512,
        "zxy",
        [(0, 384, [("h1_z", "q1", 1280)]), (384, 512, [("h1_z", "q1", 1664), ("gy_z", "o1", 0)])],
    ),
    (5 * 128, 640, "yzx", [(0, 640, [("h1_y", "q1", 640)])]),
    (0, 640, "xyz", [(0, 640, [("h1_x", "q1", 0)])]),
]
N_JOBS = len(JOBS)


def third_width(n):
    return (n // 128 + 2) // 2 * 128


def row_moves(order):
    moves = []
    for z in range(4):
        for yh in range(2):
            for c in range(2):
                base = 288 * z + 144 * yh + 72 * c
                if order == "z":
                    moves.append((base, c, 144 * z + 72 * yh, 72))
                    continue
                for x in range(4):
                    if order == "x":
                        moves.append((base + 18 * x, c, 144 * x + 36 * z + 18 * yh, 18))
                        continue
                    for yl in range(2):
                        moves.append((base + 18 * x + 9 * yl, c, 144 * (2 * yh + yl) + 36 * z + 9 * x, 9))
    return moves


def second_rows(axes, second, third):
    if axes == "zxy":
        return 72 * (third // 2) + 18 * second + 9 * (third % 2)
    if axes == "yzx":
        return 36 * second + 9 * third
    return 36 * third + 9 * second


def nn(a, b):
    return jnp.dot(a, b, preferred_element_type=F32)


def nt(a, b):
    return lax.dot_general(a, b, (((1,), (1,)), ((), ())), preferred_element_type=F32)


def tn(a, b):
    return lax.dot_general(a, b, (((0,), (0,)), ((), ())), preferred_element_type=F32)


def left_64(x):
    return pltpu.roll(x, x.shape[1] - 64, 1)


def right_64(x):
    return pltpu.roll(x, 64, 1)


def lane_mask(lo, hi, a, b):
    lane = lax.broadcasted_iota(jnp.int32, (1, b - a), 1) + a
    return (lane >= lo) & (lane < hi)


def add_head(tiles, head, value):
    lo, hi, a, b = HEAD_WINDOWS[head]
    for j in range(a // 128, b // 128):
        piece = value[:, j * 128 - a : (j + 1) * 128 - a]
        mask = lane_mask(lo, hi, j * 128, (j + 1) * 128)
        old = jnp.zeros_like(piece) if tiles[j] is None else tiles[j]
        tiles[j] = jnp.where(mask, piece, old)


def first_part(tiles):
    moved = right_64(jnp.concatenate(tiles[:3], axis=1))
    return jnp.where(lane_mask(64, 384, 0, 384), moved, 0.0).astype(BF16)


def second_part(tiles):
    return left_64(jnp.concatenate(tiles[2:], axis=1))[:, :256].astype(BF16)


def attend(qkv, dqkv, kx, dkx, pn_ref, mask, after_head_4):
    out, tan = [None] * 5, [None] * 5
    for h in range(HEADS):
        lo, hi, a, b = HEAD_WINDOWS[h]
        lanes = jnp.where(lane_mask(lo, hi, a, b), 1.0, 0.0).astype(BF16)
        q = qkv[:, a:b] * lanes
        both = jnp.concatenate([q, dqkv[:, a:b] * lanes], axis=0)
        k, dk = kx[:, a:b], dkx[:, a:b]
        v, dv = qkv[:, 1152 + a : 1152 + b], dqkv[:, 1152 + a : 1152 + b]
        against_k = nt(both, k)
        e = jnp.where(mask, jnp.exp(against_k[:128] * SCALE), 0.0)
        pn = e * (1.0 / jnp.sum(e, axis=1, keepdims=True))
        pn_ref[h] = pn
        p = pn.astype(BF16)
        ds = (against_k[128:] + nt(q, dk)) * SCALE
        dp = (pn * (ds - jnp.sum(pn * ds, axis=1, keepdims=True))).astype(BF16)
        against_v = nn(jnp.concatenate([p, dp], axis=0), v)
        add_head(out, h, against_v[:128])
        add_head(tan, h, against_v[128:] + nn(p, dv))
        if h == 4:
            after_head_4(out, tan)
    return out, tan


def attend_back(qkv, kx, pn_ref, go, grad_ref, after_head_4):
    gq, gk, gv = [None] * 5, [None] * 5, [None] * 5
    for h in range(HEADS):
        lo, hi, a, b = HEAD_WINDOWS[h]
        lanes = jnp.where(lane_mask(lo, hi, a, b), 1.0, 0.0).astype(BF16)
        gow = go[:, a:b]
        gp = nt(gow * lanes, qkv[:, 1152 + a : 1152 + b]).astype(BF16).astype(F32)
        pn = pn_ref[h]
        gs = (pn * (gp - jnp.sum(gp * pn, axis=1, keepdims=True)) * SCALE).astype(BF16)
        add_head(gq, h, nn(gs, kx[:, a:b]))
        add_head(gk, h, tn(gs, qkv[:, a:b]))
        add_head(gv, h, tn(pn.astype(BF16), gow))
        if h == 4:
            after_head_4()
    gkr = right_64(jnp.concatenate(gk, axis=1))
    for j in range(4):
        grad_ref[:, j * 128 : (j + 1) * 128] = gq[j].astype(BF16)
    grad_ref[:, 512:640] = (gq[4] + gkr[:, :128]).astype(BF16)
    grad_ref[:, 640:1152] = gkr[:, 128:].astype(BF16)
    for j in range(5):
        grad_ref[:, 1152 + j * 128 : 1280 + j * 128] = gv[j].astype(BF16)


def norm_parts(x):
    centred = x - jnp.mean(x, axis=-1, keepdims=True)
    rstd = lax.rsqrt(jnp.mean(centred * centred, axis=-1, keepdims=True) + 1e-06)
    return centred * rstd, rstd


def norm_tangent(normed, rstd, dx):
    return rstd * (
        dx
        - jnp.mean(dx, axis=-1, keepdims=True)
        - normed * jnp.mean(normed * dx, axis=-1, keepdims=True)
    )


def shape_list():
    v = pltpu.VMEM
    dma = pltpu.SemaphoreType.DMA
    scratch = {
        "wp": v((D, 4608), BF16),
        "wd": v((D, 4608), BF16),
        "h1": v((128, D), BF16),
        "qkv1": v((128, QKV), BF16),
        "dqkv1": v((128, QKV), BF16),
        "kx1": v((128, OUT), BF16),
        "dkx": v((128, OUT), BF16),
        "pn1": v((HEADS, 128, 128), F32),
        "qkv2": v((128, QKV), BF16),
        "dqkv2": v((128, QKV), BF16),
        "kx2": v((128, OUT), BF16),
        "pn2": v((HEADS, 128, 128), F32),
        "go": v((128, OUT), BF16),
        "clips_s": v((8, 16, D), BF16),
        "clips_r": v((8, 16, D), BF16),
        "attn_s": v((8, 16, 768), BF16),
        "attn_r": v((8, 16, 768), BF16),
        "attn2_s": v((8, 16, 512), BF16),
        "attn2_r": v((8, 16, 512), BF16),
        "go_s": v((8, 16, OUT), BF16),
        "go_r": v((8, 16, OUT), BF16),
        "tan_s": v((8, 16, D), BF16),
        "tan_r": v((8, 16, D), BF16),
        "lt": v((D, 128), F32),
        "lts": v((2, 576, 128), F32),
        "left": v((len(LEFTS), 576, 256), BF16),
        "left_s": v((len(LEFTS), 576, 128), BF16),
    }
    for name, width in RIGHTS.items():
        scratch["r_" + name] = v((256, width), BF16)
    for i, (_, n, _, _) in enumerate(JOBS):
        scratch[f"p{i}"] = v((4, 144, n), BF16)
        scratch[f"u{i}"] = v((144, n), BF16)
        scratch[f"m{i}"] = v((144, n), BF16)
        scratch[f"v{i}"] = v((2, 144, n), BF16)
        scratch[f"s2_{i}"] = v((4, 32, n + 128), BF16)
        scratch[f"v2_{i}"] = v((3, 32, n + 128), BF16)
        scratch[f"s3_{i}"] = v((4, 16, third_width(n)), BF16)
        scratch[f"v3_{i}"] = v((3, 16, third_width(n)), BF16)
    scratch["acc1"] = v((144, 896), F32)
    scratch["acc2"] = v((40, 896), F32)
    scratch["pad2"] = v((40, 896), F32)
    scratch["ext2"] = v((32, 128), F32)
    scratch["pad3"] = v((16, 512), F32)
    scratch["w_sem"] = dma((8,))
    scratch["a_send"] = dma((5, 7))
    scratch["a_recv"] = dma((5, 7))
    scratch["c_send"] = dma((len(LEFTS) + len(RIGHTS),))
    scratch["c_recv"] = dma((len(LEFTS) + len(RIGHTS),))
    scratch["rs_send"] = dma((N_JOBS, 12))
    scratch["rs_recv"] = dma((N_JOBS, 12))
    return scratch


SCRATCH = shape_list()


def kernel(clips_ref, params_ref, direction_ref, tan_ref, gnv_ref, *scratch_refs):
    s = dict(zip(SCRATCH, scratch_refs))
    dp, fr = lax.axis_index("dp"), lax.axis_index("frame")
    core, y_hi, z = dp % 2, dp // 2 % 2, dp // 4
    x, y_lo = fr // 2, fr % 2
    where = {"z": z, "y": 2 * y_hi + y_lo, "x": x}

    def device(at, c):
        return (at["z"] * 4 + at["y"] // 2 * 2 + c, at["x"] * 2 + at["y"] % 2)

    def along(axis, k):
        at = dict(where)
        at[axis] = (at[axis] + k) % 4
        return device(at, core)

    partner = (dp + 1 - 2 * core, fr)

    def remote(src, dst, send, recv, to):
        copy = pltpu.make_async_remote_copy(
            src_ref=src, dst_ref=dst, send_sem=send, recv_sem=recv, device_id=to, device_id_type=MESH
        )
        copy.start()
        sent.append(copy)
        return copy

    sent = []

    loads = []
    for i, (lo, hi) in enumerate([(0, 1792), (1792, 2304), (2304, 4096), (4096, 4608)]):
        pair = []
        for j, (src, dst) in enumerate([(params_ref, s["wp"]), (direction_ref, s["wd"])]):
            copy = pltpu.make_async_copy(src.at[:, lo:hi], dst.at[:, lo:hi], s["w_sem"].at[2 * i + j])
            copy.start()
            pair.append(copy)
        loads.append(pair)

    def loaded(i):
        for copy in loads[i]:
            copy.wait()

    barrier = pltpu.get_barrier_semaphore()
    peers = [along(axis, k) for axis in "zyx" for k in (1, 2, 3)]
    peers += [(dp, (x + k) % 4 * 2 + 1 - y_lo) for k in (1, 2, 3)]
    peers.append(partner)
    for peer in peers:
        pl.semaphore_signal(barrier, inc=1, device_id=peer, device_id_type=MESH)

    natural = clips_ref[...].astype(F32)
    tokens = jnp.concatenate(
        [natural[f, 8 * t : 8 * t + 8] for t in range(8) for f in range(2)], axis=0
    )
    s["clips_s"][...] = tokens.astype(BF16).reshape(8, 16, D)
    h1f, _ = norm_parts(tokens)
    s["h1"][...] = h1f.astype(BF16)

    pl.semaphore_wait(barrier, len(peers))

    def frame_exchange(which, src, dst):
        copies = []
        for k in range(1, 8):
            t = (fr + k) % 8
            copies.append(
                remote(src.at[t], dst.at[fr], s["a_send"].at[which, k - 1], s["a_recv"].at[which, k - 1], (dp, t))
            )
        dst[fr] = src[fr]
        return copies

    def arrived(copies):
        for copy in copies:
            copy.wait_recv()

    clips_copies = frame_exchange(0, s["clips_s"], s["clips_r"])

    left_copies = {}

    def prepare_left(value, names):
        s["lt"][...] = value.T
        for name in names:
            i = LEFTS.index(name)
            for src, c, dst, rows in row_moves(name[-1]):
                s["lts"][c, dst : dst + rows, :] = s["lt"][src : src + rows, :]
            s["left"][i, :, 0:128] = s["lts"][core].astype(BF16)
            s["left_s"][i] = s["lts"][1 - core].astype(BF16)
            left_copies[name] = remote(
                s["left_s"].at[i], s["left"].at[i, :, pl.ds(128, 128)], s["c_send"].at[i], s["c_recv"].at[i], partner
            )

    right_copies = {}

    def share_right(name):
        i = len(LEFTS) + list(RIGHTS).index(name)
        ref = s["r_" + name]
        right_copies[name] = remote(
            ref.at[pl.ds(0, 128)], ref.at[pl.ds(128, 128)], s["c_send"].at[i], s["c_recv"].at[i], partner
        )

    s["ext2"][...] = jnp.zeros_like(s["ext2"])
    s["pad3"][...] = jnp.zeros_like(s["pad3"])
    flight = {}
    shared = []

    def product(job):
        _, n, axes, segments = JOBS[job]
        needed = [name for _, _, terms in segments for left, right, _ in terms for name in (left, right)]
        for name in needed:
            copies = left_copies if name in left_copies else right_copies
            if name not in shared:
                copies[name].wait_recv()
                shared.append(name)
        part, first_in, ready = s[f"p{job}"], s[f"u{job}"], s[f"v{job}"]
        for lo, hi, terms in segments:
            acc = None
            for left, right, at in terms:
                term = nn(s["left"][LEFTS.index(left)], s["r_" + right][:, at : at + hi - lo])
                acc = term if acc is None else acc + term
            part[:, :, lo:hi] = acc.astype(BF16).reshape(4, 144, hi - lo)
        here = where[axes[0]]
        right, left = along(axes[0], 1), along(axes[0], 3)
        ahead, behind, across = (here + 1) % 4, (here + 3) % 4, (here + 2) % 4
        flight[job] = [
            remote(src.at[pl.ds(at, rows)], dst.at[pl.ds(at, rows)], s["rs_send"].at[job, i], s["rs_recv"].at[job, i], to)
            for i, (src, dst, at, rows, to) in enumerate(
                [
                    (part.at[across], first_in, 0, 80, right),
                    (part.at[across], first_in, 80, 64, left),
                    (part.at[ahead], ready.at[0], 80, 64, right),
                    (part.at[behind], ready.at[1], 0, 80, left),
                ]
            )
        ]

    def merge(job):
        here = where[JOBS[job][2][0]]
        part, first_in, merged, ready = s[f"p{job}"], s[f"u{job}"], s[f"m{job}"], s[f"v{job}"]
        for i, k, at, rows in [(0, 1, 0, 80), (1, 3, 80, 64)]:
            flight[job][i].wait_recv()
            own = part[(here + k) % 4, at : at + rows].astype(F32)
            merged[at : at + rows] = (own + first_in[at : at + rows].astype(F32)).astype(BF16)
            flight[job].append(
                remote(
                    merged.at[pl.ds(at, rows)],
                    ready.at[i, pl.ds(at, rows)],
                    s["rs_send"].at[job, 4 + i],
                    s["rs_recv"].at[job, 4 + i],
                    along(JOBS[job][2][0], k),
                )
            )

    def scatter(job, stage, src, dst):
        axis = JOBS[job][2][stage]
        flight[job] = []
        for k in (1, 2, 3):
            i = 3 + 3 * stage + k - 1
            flight[job].append(
                remote(
                    src.at[(where[axis] + k) % 4],
                    dst.at[k - 1],
                    s["rs_send"].at[job, i],
                    s["rs_recv"].at[job, i],
                    along(axis, k),
                )
            )

    def second_stage(job):
        _, n, axes, _ = JOBS[job]
        arrived(flight[job][2:])
        part, ready = s[f"p{job}"], s[f"v{job}"]
        s["acc1"][:, :n] = part[where[axes[0]]].astype(F32) + ready[0].astype(F32) + ready[1].astype(F32)
        for second in range(4):
            for third in range(4):
                at = second_rows(axes, second, third)
                s["pad2"][9 * third : 9 * third + 9, :n] = s["acc1"][at : at + 9, :n]
            for j in range(n // 128):
                s["ext2"][4 * j : 4 * j + 4] = s["pad2"][32:36, 128 * j : 128 * j + 128]
            s[f"s2_{job}"][second, :, :n] = s["pad2"][0:32, :n].astype(BF16)
            s[f"s2_{job}"][second, :, n:] = s["ext2"][...].astype(BF16)
        scatter(job, 1, s[f"s2_{job}"], s[f"v2_{job}"])

    def total(job, stage, src, dst):
        arrived(flight[job])
        mine = src[where[JOBS[job][2][stage]]].astype(F32)
        return mine + dst[0].astype(F32) + dst[1].astype(F32) + dst[2].astype(F32)

    def third_stage(job):
        n = JOBS[job][1]
        tiles, width = n // 128, third_width(n)
        sums = total(job, 1, s[f"s2_{job}"], s[f"v2_{job}"])
        s["acc2"][0:32, :n] = sums[:, :n]
        s["ext2"][...] = sums[:, n:]
        for j in range(tiles):
            s["acc2"][32:36, 128 * j : 128 * j + 128] = s["ext2"][4 * j : 4 * j + 4]
        for third in range(4):
            for j in range(tiles):
                lanes, at, ninth = slice(128 * j, 128 * j + 128), 128 * (j // 2), 128 * (tiles // 2)
                s["pad3"][8 * (j % 2) : 8 * (j % 2) + 8, at : at + 128] = s["acc2"][9 * third : 9 * third + 8, lanes]
                row = 8 * (tiles % 2) + j
                s["pad3"][row : row + 1, ninth : ninth + 128] = s["acc2"][9 * third + 8 : 9 * third + 9, lanes]
            s[f"s3_{job}"][third] = s["pad3"][:, :width].astype(BF16)
        scatter(job, 2, s[f"s3_{job}"], s[f"v3_{job}"])

    def finish(job):
        first, n, _, _ = JOBS[job]
        tiles, width = n // 128, third_width(n)
        s["pad3"][:, :width] = total(job, 2, s[f"s3_{job}"], s[f"v3_{job}"])
        for j in range(tiles):
            lanes, at, ninth = slice(first + 128 * j, first + 128 * j + 128), 128 * (j // 2), 128 * (tiles // 2)
            row = 8 * (tiles % 2) + j
            gnv_ref[0:8, lanes] = s["pad3"][8 * (j % 2) : 8 * (j % 2) + 8, at : at + 128]
            gnv_ref[8:9, lanes] = s["pad3"][row : row + 1, ninth : ninth + 128]

    loaded(0)
    for lo in range(0, QKV, 256):
        s["qkv1"][:, lo : lo + 256] = nn(s["h1"][...], s["wp"][:, lo : lo + 256]).astype(BF16)
        s["dqkv1"][:, lo : lo + 256] = nn(s["h1"][...], s["wd"][:, lo : lo + 256]).astype(BF16)

    def align_keys(qkv, kx):
        kx[...] = left_64(qkv[:, 512:1152].astype(F32)).astype(BF16)

    row = lax.broadcasted_iota(jnp.int32, (128, 128), 0)
    col = lax.broadcasted_iota(jnp.int32, (128, 128), 1)
    same_frame = row // 8 % 2 == col // 8 % 2
    same_patch = row % 8 == col % 8
    align_keys(s["qkv1"], s["kx1"])
    align_keys(s["dqkv1"], s["dkx"])
    attn_copies = []

    def send_first(out, tan):
        s["attn_s"][:, :, 0:384] = first_part(out).reshape(8, 16, 384)
        s["attn_s"][:, :, 384:768] = first_part(tan).reshape(8, 16, 384)
        attn_copies.extend(frame_exchange(1, s["attn_s"], s["attn_r"]))

    o1, do1 = attend(s["qkv1"], s["dqkv1"], s["kx1"], s["dkx"], s["pn1"], same_frame, send_first)
    s["attn2_s"][:, :, 0:256] = second_part(o1).reshape(8, 16, 256)
    s["attn2_s"][:, :, 256:512] = second_part(do1).reshape(8, 16, 256)
    attn_copies.extend(frame_exchange(4, s["attn2_s"], s["attn2_r"]))

    prepare_left(h1f.astype(BF16).astype(F32), ["h1_z", "h1_y", "h1_x"])

    arrived(clips_copies)
    loaded(1)
    arrived(attn_copies)
    clips_p = s["clips_r"][...].reshape(128, D).astype(F32)
    parts = s["attn_r"][...].reshape(128, 768), s["attn2_r"][...].reshape(128, 512)
    o1x = jnp.concatenate([parts[0][:, :384], parts[1][:, :256]], axis=1)
    do1x = jnp.concatenate([parts[0][:, 384:], parts[1][:, 256:]], axis=1)
    s["r_o1"][0:128, :] = o1x
    share_right("o1")
    s_out, v_sout = s["wp"][:, S_OUT : S_OUT + OUT], s["wd"][:, S_OUT : S_OUT + OUT]
    through = nt(jnp.concatenate([o1x, do1x], axis=0), s_out)
    y = (clips_p + through[:128]).astype(BF16).astype(F32)
    dy = (through[128:] + nt(o1x, v_sout)).astype(BF16).astype(F32)
    h2f, rstd = norm_parts(y)
    h2 = h2f.astype(BF16)
    h2_both = jnp.concatenate([h2, norm_tangent(h2f, rstd, dy).astype(BF16)], axis=0)
    prepare_left(h2.astype(F32), ["h2_y", "h2_x"])
    loaded(2)
    for lo in range(0, QKV, 256):
        wp = s["wp"][:, T_QKV + lo : T_QKV + lo + 256]
        wd = s["wd"][:, T_QKV + lo : T_QKV + lo + 256]
        through = nn(h2_both, wp)
        s["qkv2"][:, lo : lo + 256] = through[:128].astype(BF16)
        s["dqkv2"][:, lo : lo + 256] = (through[128:] + nn(h2, wd)).astype(BF16)
    align_keys(s["qkv2"], s["kx2"])
    align_keys(s["dqkv2"], s["dkx"])
    o2, do2 = attend(s["qkv2"], s["dqkv2"], s["kx2"], s["dkx"], s["pn2"], same_patch, lambda *_: None)
    o2x = right_64(jnp.concatenate(o2, axis=1)).astype(BF16)
    do2x = right_64(jnp.concatenate(do2, axis=1)).astype(BF16)
    s["r_o2"][0:128, :] = o2x
    share_right("o2")
    loaded(3)
    t_out, v_tout = s["wp"][:, T_OUT : T_OUT + OUT], s["wd"][:, T_OUT : T_OUT + OUT]
    tangent = (dy + nt(do2x, t_out) + nt(o2x, v_tout)).astype(BF16)
    s["tan_s"][...] = tangent.reshape(8, 16, D)
    tan_copies = frame_exchange(3, s["tan_s"], s["tan_r"])
    g = (tangent.astype(F32) * (16384 ** (-0.5))).astype(BF16)
    prepare_left(g.astype(F32), ["g_z", "g_x"])
    s["go"][...] = left_64(nn(g, t_out)).astype(BF16)
    attend_back(s["qkv2"], s["kx2"], s["pn2"], s["go"], s["r_q2"].at[pl.ds(0, 128)], lambda: product(0))
    share_right("q2")
    gq2 = s["r_q2"][0:128, :]
    gh2 = nt(gq2, s["wp"][:, T_QKV : T_QKV + QKV])
    gy = (g.astype(F32) + norm_tangent(h2f, rstd, gh2)).astype(BF16)
    s["go_s"][...] = nn(gy, s_out).astype(BF16).reshape(8, 16, OUT)
    go_copies = frame_exchange(2, s["go_s"], s["go_r"])

    prepare_left(gy.astype(F32), ["gy_z"])
    product(1)
    product(2)
    product(3)
    merge(0)

    arrived(go_copies)
    s["go"][...] = left_64(s["go_r"][...].reshape(128, OUT).astype(F32)).astype(BF16)
    attend_back(s["qkv1"], s["kx1"], s["pn1"], s["go"], s["r_q1"].at[pl.ds(0, 128)], lambda: None)
    share_right("q1")

    merge(1)
    merge(2)
    merge(3)
    product(4)
    product(5)
    product(6)
    arrived(tan_copies)
    tan = s["tan_r"][...].reshape(128, D).astype(F32)
    for f in range(2):
        tan_ref[f] = jnp.concatenate(
            [tan[16 * t + 8 * f : 16 * t + 8 * f + 8] for t in range(8)], axis=0
        ).astype(BF16)
    second_stage(0)
    second_stage(1)
    second_stage(2)
    second_stage(3)
    for job in (5, 6, 4):
        merge(job)
    for job in (0, 1, 2, 3):
        third_stage(job)
    for job in (5, 6, 4):
        second_stage(job)
    for job in (0, 1, 2, 3):
        finish(job)
    for job in (5, 6, 4):
        third_stage(job)
    for job in (5, 6, 4):
        finish(job)

    for copy in sent:
        copy.wait_send()


def place(tan_in, gnv_in, tan_out, gnv_out):
    tan_out[...] = tan_in[...]
    gnv_out[...] = gnv_in[...]


def body(clips, params, direction):
    tangent, gnv = pl.pallas_call(
        kernel,
        out_shape=(
            jax.ShapeDtypeStruct((2, 64, D), BF16),
            jax.ShapeDtypeStruct((9, 4608), F32),
        ),
        in_specs=[
            pl.BlockSpec(memory_space=pltpu.VMEM),
            pl.BlockSpec(memory_space=pl.ANY),
            pl.BlockSpec(memory_space=pl.ANY),
        ],
        out_specs=(pl.BlockSpec(memory_space=pltpu.VMEM), pl.BlockSpec(memory_space=pltpu.VMEM)),
        scratch_shapes=list(SCRATCH.values()),
        compiler_params=pltpu.CompilerParams(
            collective_id=0, has_side_effects=True, vmem_limit_bytes=62 * 2**20
        ),
    )(clips[0], params, direction)
    tangent, gnv = pl.pallas_call(
        place,
        out_shape=(
            jax.ShapeDtypeStruct((2, 64, D), BF16),
            jax.ShapeDtypeStruct((9, 4608), F32),
        ),
        in_specs=[pl.BlockSpec(memory_space=pltpu.VMEM)] * 2,
        out_specs=(pl.BlockSpec(memory_space=pltpu.VMEM),) * 2,
    )(tangent, gnv)
    return tangent[None], gnv


def solution(mesh):
    in_specs = (P("dp", "frame", None, None), P(), P())
    out_specs = (P("dp", "frame", None, None), P(("dp", "frame"), None))
    return jax.shard_map(body, mesh=mesh, in_specs=in_specs, out_specs=out_specs, check_vma=False)
```

```python
import jax
import jax.numpy as jnp
from jax import lax
from jax.experimental import pallas as pl
from jax.experimental.pallas import tpu as pltpu
from jax.sharding import PartitionSpec as P

MESH = pl.DeviceIdType.MESH
F32 = jnp.float32
BF16 = jnp.bfloat16

D = 1152
HD = 72
HEADS = 8
QKV = 1792
OUT = 640
SCALE = HD ** (-0.5)

S_QKV, S_OUT, T_QKV, T_OUT = 0, 1664, 2304, 3968

HEAD_WINDOWS = [
    (h * HD, (h + 1) * HD, h * HD // 128 * 128, -(-(h + 1) * HD // 128) * 128)
    for h in range(HEADS)
]

ALL = [(0, 1, 2, 3, 4, 5, 6, 7)]
FIVE_THREE = [(0, 1, 2, 3, 4), (5, 6, 7)]

LEFTS = ["g_z", "g_x", "h2_y", "h2_x", "gy_z", "h1_z", "h1_y", "h1_x"]
RIGHTS = {"q1": QKV, "o1": OUT, "q2": QKV, "o2": OUT}

JOBS = [
    (32 * 128, 512, "zxy", [(0, 512, [("g_z", "o2", 128)])]),
    (18 * 128, 896, "yzx", [(0, 896, [("h2_y", "q2", 0)])]),
    (
        25 * 128,
        896,
        "xyz",
        [(0, 768, [("h2_x", "q2", 896)]), (768, 896, [("h2_x", "q2", 1664), ("g_x", "o2", 0)])],
    ),
    (14 * 128, 512, "zxy", [(0, 512, [("gy_z", "o1", 128)])]),
    (
        10 * 128,
        512,
        "zxy",
        [(0, 384, [("h1_z", "q1", 1280)]), (384, 512, [("h1_z", "q1", 1664), ("gy_z", "o1", 0)])],
    ),
    (5 * 128, 640, "yzx", [(0, 640, [("h1_y", "q1", 640)])]),
    (0, 640, "xyz", [(0, 640, [("h1_x", "q1", 0)])]),
]
N_JOBS = len(JOBS)


def third_width(n):
    return (n // 128 + 2) // 2 * 128


def row_moves(order):
    moves = []
    for z in range(4):
        for yh in range(2):
            for c in range(2):
                base = 288 * z + 144 * yh + 72 * c
                if order == "z":
                    moves.append((base, c, 144 * z + 72 * yh, 72))
                    continue
                for x in range(4):
                    if order == "x":
                        moves.append((base + 18 * x, c, 144 * x + 36 * z + 18 * yh, 18))
                        continue
                    for yl in range(2):
                        moves.append((base + 18 * x + 9 * yl, c, 144 * (2 * yh + yl) + 36 * z + 9 * x, 9))
    return moves


def second_rows(axes, second, third):
    if axes == "zxy":
        return 72 * (third // 2) + 18 * second + 9 * (third % 2)
    if axes == "yzx":
        return 36 * second + 9 * third
    return 36 * third + 9 * second


def nn(a, b):
    return jnp.dot(a, b, preferred_element_type=F32)


def nt(a, b):
    return lax.dot_general(a, b, (((1,), (1,)), ((), ())), preferred_element_type=F32)


def tn(a, b):
    return lax.dot_general(a, b, (((0,), (0,)), ((), ())), preferred_element_type=F32)


def left_64(x):
    return pltpu.roll(x, x.shape[1] - 64, 1)


def right_64(x):
    return pltpu.roll(x, 64, 1)


def lane_mask(lo, hi, a, b):
    lane = lax.broadcasted_iota(jnp.int32, (1, b - a), 1) + a
    return (lane >= lo) & (lane < hi)


def add_head(tiles, head, value):
    lo, hi, a, b = HEAD_WINDOWS[head]
    for j in range(a // 128, b // 128):
        piece = value[:, j * 128 - a : (j + 1) * 128 - a]
        mask = lane_mask(lo, hi, j * 128, (j + 1) * 128)
        old = jnp.zeros_like(piece) if tiles[j] is None else tiles[j]
        tiles[j] = jnp.where(mask, piece, old)


def first_part(tiles):
    moved = right_64(jnp.concatenate(tiles[:3], axis=1))
    return jnp.where(lane_mask(64, 384, 0, 384), moved, 0.0).astype(BF16)


def second_part(tiles):
    return left_64(jnp.concatenate(tiles[2:], axis=1))[:, :256].astype(BF16)


def attend(qkv, dqkv, kx, dkx, pn_ref, mask, groups, after_head_4=lambda *_: None):
    out, tan = [None] * 5, [None] * 5
    for group in groups:
        against_k, dk_part, ps = {}, {}, {}
        for h in group:
            lo, hi, a, b = HEAD_WINDOWS[h]
            lanes = jnp.where(lane_mask(lo, hi, a, b), 1.0, 0.0).astype(BF16)
            q = qkv[:, a:b] * lanes
            both = jnp.concatenate([q, dqkv[:, a:b] * lanes], axis=0)
            against_k[h] = nt(both, kx[:, a:b])
            dk_part[h] = nt(q, dkx[:, a:b])
        for h in group:
            e = jnp.where(mask, jnp.exp(against_k[h][:128] * SCALE), 0.0)
            pn = e * (1.0 / jnp.sum(e, axis=1, keepdims=True))
            pn_ref[h] = pn
            ds = (against_k[h][128:] + dk_part[h]) * SCALE
            dp = pn * (ds - jnp.sum(pn * ds, axis=1, keepdims=True))
            ps[h] = jnp.concatenate([pn.astype(BF16), dp.astype(BF16)], axis=0)
        for h in group:
            lo, hi, a, b = HEAD_WINDOWS[h]
            against_v = nn(ps[h], qkv[:, 1152 + a : 1152 + b])
            add_head(out, h, against_v[:128])
            add_head(tan, h, against_v[128:] + nn(ps[h][:128], dqkv[:, 1152 + a : 1152 + b]))
            if h == 4:
                after_head_4(out, tan)
    return out, tan


def attend_back(qkv, kx, pn_ref, go, grad_ref, groups, after_head_4=lambda: None):
    gq, gk, gv = [None] * 5, [None] * 5, [None] * 5
    for group in groups:
        gp, gs, gow = {}, {}, {}
        for h in group:
            lo, hi, a, b = HEAD_WINDOWS[h]
            lanes = jnp.where(lane_mask(lo, hi, a, b), 1.0, 0.0).astype(BF16)
            gow[h] = go[:, a:b]
            gp[h] = nt(gow[h] * lanes, qkv[:, 1152 + a : 1152 + b])
        for h in group:
            pn = pn_ref[h]
            rounded = gp[h].astype(BF16).astype(F32)
            gs[h] = (pn * (rounded - jnp.sum(rounded * pn, axis=1, keepdims=True)) * SCALE).astype(BF16)
        for h in group:
            lo, hi, a, b = HEAD_WINDOWS[h]
            add_head(gv, h, tn(pn_ref[h].astype(BF16), gow[h]))
            add_head(gq, h, nn(gs[h], kx[:, a:b]))
            add_head(gk, h, tn(gs[h], qkv[:, a:b]))
            if h == 4:
                after_head_4()
    gkr = right_64(jnp.concatenate(gk, axis=1))
    for j in range(4):
        grad_ref[:, j * 128 : (j + 1) * 128] = gq[j].astype(BF16)
    grad_ref[:, 512:640] = (gq[4] + gkr[:, :128]).astype(BF16)
    grad_ref[:, 640:1152] = gkr[:, 128:].astype(BF16)
    for j in range(5):
        grad_ref[:, 1152 + j * 128 : 1280 + j * 128] = gv[j].astype(BF16)


def norm_parts(x):
    centred = x - jnp.mean(x, axis=-1, keepdims=True)
    rstd = lax.rsqrt(jnp.mean(centred * centred, axis=-1, keepdims=True) + 1e-06)
    return centred * rstd, rstd


def norm_tangent(normed, rstd, dx):
    return rstd * (
        dx
        - jnp.mean(dx, axis=-1, keepdims=True)
        - normed * jnp.mean(normed * dx, axis=-1, keepdims=True)
    )


def shape_list():
    v = pltpu.VMEM
    dma = pltpu.SemaphoreType.DMA
    scratch = {
        "wp": v((D, 4608), BF16),
        "wd": v((D, 4608), BF16),
        "h1": v((128, D), BF16),
        "qkv1": v((128, QKV), BF16),
        "dqkv1": v((128, QKV), BF16),
        "kx1": v((128, OUT), BF16),
        "dkx": v((128, OUT), BF16),
        "pn1": v((HEADS, 128, 128), F32),
        "qkv2": v((128, QKV), BF16),
        "dqkv2": v((128, QKV), BF16),
        "kx2": v((128, OUT), BF16),
        "pn2": v((HEADS, 128, 128), F32),
        "go": v((128, OUT), BF16),
        "clips_s": v((8, 16, D), BF16),
        "clips_r": v((8, 16, D), BF16),
        "attn_s": v((8, 16, 768), BF16),
        "attn_r": v((8, 16, 768), BF16),
        "attn2_s": v((8, 16, 512), BF16),
        "attn2_r": v((8, 16, 512), BF16),
        "go_s": v((8, 16, OUT), BF16),
        "go_r": v((8, 16, OUT), BF16),
        "tan_s": v((8, 16, D), BF16),
        "tan_r": v((8, 16, D), BF16),
        "lt": v((D, 128), F32),
        "lts": v((2, 576, 128), F32),
        "left": v((len(LEFTS), 576, 256), BF16),
        "left_s": v((len(LEFTS), 576, 128), BF16),
    }
    for name, width in RIGHTS.items():
        scratch["r_" + name] = v((256, width), BF16)
    for i, (_, n, _, _) in enumerate(JOBS):
        scratch[f"p{i}"] = v((4, 144, n), BF16)
        scratch[f"u{i}"] = v((144, n), BF16)
        scratch[f"m{i}"] = v((144, n), BF16)
        scratch[f"v{i}"] = v((2, 144, n), BF16)
        scratch[f"s2_{i}"] = v((4, 32, n + 128), BF16)
        scratch[f"v2_{i}"] = v((3, 32, n + 128), BF16)
        scratch[f"s3_{i}"] = v((4, 16, third_width(n)), BF16)
        scratch[f"v3_{i}"] = v((3, 16, third_width(n)), BF16)
    scratch["acc1"] = v((144, 896), F32)
    scratch["acc2"] = v((40, 896), F32)
    scratch["pad2"] = v((40, 896), F32)
    scratch["ext2"] = v((32, 128), F32)
    scratch["pad3"] = v((16, 512), F32)
    scratch["w_sem"] = dma((10,))
    scratch["a_send"] = dma((5, 7))
    scratch["a_recv"] = dma((5, 7))
    scratch["c_send"] = dma((len(LEFTS) + len(RIGHTS),))
    scratch["c_recv"] = dma((len(LEFTS) + len(RIGHTS),))
    scratch["rs_send"] = dma((N_JOBS, 12))
    scratch["rs_recv"] = dma((N_JOBS, 12))
    return scratch


SCRATCH = shape_list()


def kernel(clips_ref, params_ref, direction_ref, tan_ref, gnv_ref, *scratch_refs):
    s = dict(zip(SCRATCH, scratch_refs))
    dp, fr = lax.axis_index("dp"), lax.axis_index("frame")
    core, y_hi, z = dp % 2, dp // 2 % 2, dp // 4
    x, y_lo = fr // 2, fr % 2
    where = {"z": z, "y": 2 * y_hi + y_lo, "x": x}

    def device(at, c):
        return (at["z"] * 4 + at["y"] // 2 * 2 + c, at["x"] * 2 + at["y"] % 2)

    def along(axis, k):
        at = dict(where)
        at[axis] = (at[axis] + k) % 4
        return device(at, core)

    partner = (dp + 1 - 2 * core, fr)

    def remote(src, dst, send, recv, to):
        copy = pltpu.make_async_remote_copy(
            src_ref=src, dst_ref=dst, send_sem=send, recv_sem=recv, device_id=to, device_id_type=MESH
        )
        copy.start()
        sent.append(copy)
        return copy

    sent = []

    loads = []
    spans = [(0, 1024), (1024, 1792), (1792, 2304), (2304, 4096), (4096, 4608)]
    for i, (lo, hi) in enumerate(spans):
        pair = []
        for j, (src, dst) in enumerate([(params_ref, s["wp"]), (direction_ref, s["wd"])]):
            copy = pltpu.make_async_copy(src.at[:, lo:hi], dst.at[:, lo:hi], s["w_sem"].at[2 * i + j])
            copy.start()
            pair.append(copy)
        loads.append(pair)

    def loaded(i):
        for copy in loads[i]:
            copy.wait()

    barrier = pltpu.get_barrier_semaphore()
    peers = [along(axis, k) for axis in "zyx" for k in (1, 2, 3)]
    peers += [(dp, (x + k) % 4 * 2 + 1 - y_lo) for k in (1, 2, 3)]
    peers.append(partner)
    for peer in peers:
        pl.semaphore_signal(barrier, inc=1, device_id=peer, device_id_type=MESH)

    natural = clips_ref[...].astype(F32)
    tokens = jnp.concatenate(
        [natural[f, 8 * t : 8 * t + 8] for t in range(8) for f in range(2)], axis=0
    )
    s["clips_s"][...] = tokens.astype(BF16).reshape(8, 16, D)
    h1f, _ = norm_parts(tokens)
    s["h1"][...] = h1f.astype(BF16)

    pl.semaphore_wait(barrier, len(peers))

    def frame_exchange(which, src, dst):
        copies = []
        for k in range(1, 8):
            t = (fr + k) % 8
            copies.append(
                remote(src.at[t], dst.at[fr], s["a_send"].at[which, k - 1], s["a_recv"].at[which, k - 1], (dp, t))
            )
        dst[fr] = src[fr]
        return copies

    def arrived(copies):
        for copy in copies:
            copy.wait_recv()

    clips_copies = frame_exchange(0, s["clips_s"], s["clips_r"])

    left_copies = {}

    def prepare_left(value, names):
        s["lt"][...] = value.T
        for name in names:
            i = LEFTS.index(name)
            for src, c, dst, rows in row_moves(name[-1]):
                s["lts"][c, dst : dst + rows, :] = s["lt"][src : src + rows, :]
            s["left"][i, :, 0:128] = s["lts"][core].astype(BF16)
            s["left_s"][i] = s["lts"][1 - core].astype(BF16)
            left_copies[name] = remote(
                s["left_s"].at[i], s["left"].at[i, :, pl.ds(128, 128)], s["c_send"].at[i], s["c_recv"].at[i], partner
            )

    right_copies = {}

    def share_right(name):
        i = len(LEFTS) + list(RIGHTS).index(name)
        ref = s["r_" + name]
        right_copies[name] = remote(
            ref.at[pl.ds(0, 128)], ref.at[pl.ds(128, 128)], s["c_send"].at[i], s["c_recv"].at[i], partner
        )

    s["ext2"][...] = jnp.zeros_like(s["ext2"])
    s["pad3"][...] = jnp.zeros_like(s["pad3"])
    flight = {}
    shared = []

    def product(job):
        _, n, axes, segments = JOBS[job]
        needed = [name for _, _, terms in segments for left, right, _ in terms for name in (left, right)]
        for name in needed:
            copies = left_copies if name in left_copies else right_copies
            if name not in shared:
                copies[name].wait_recv()
                shared.append(name)
        part, first_in, ready = s[f"p{job}"], s[f"u{job}"], s[f"v{job}"]
        for lo, hi, terms in segments:
            acc = None
            for left, right, at in terms:
                term = nn(s["left"][LEFTS.index(left)], s["r_" + right][:, at : at + hi - lo])
                acc = term if acc is None else acc + term
            part[:, :, lo:hi] = acc.astype(BF16).reshape(4, 144, hi - lo)
        here = where[axes[0]]
        right, left = along(axes[0], 1), along(axes[0], 3)
        ahead, behind, across = (here + 1) % 4, (here + 3) % 4, (here + 2) % 4
        flight[job] = [
            remote(src.at[pl.ds(at, rows)], dst.at[pl.ds(at, rows)], s["rs_send"].at[job, i], s["rs_recv"].at[job, i], to)
            for i, (src, dst, at, rows, to) in enumerate(
                [
                    (part.at[across], first_in, 0, 80, right),
                    (part.at[across], first_in, 80, 64, left),
                    (part.at[ahead], ready.at[0], 80, 64, right),
                    (part.at[behind], ready.at[1], 0, 80, left),
                ]
            )
        ]

    def merge(job):
        here = where[JOBS[job][2][0]]
        part, first_in, merged, ready = s[f"p{job}"], s[f"u{job}"], s[f"m{job}"], s[f"v{job}"]
        for i, k, at, rows in [(0, 1, 0, 80), (1, 3, 80, 64)]:
            flight[job][i].wait_recv()
            own = part[(here + k) % 4, at : at + rows].astype(F32)
            merged[at : at + rows] = (own + first_in[at : at + rows].astype(F32)).astype(BF16)
            flight[job].append(
                remote(
                    merged.at[pl.ds(at, rows)],
                    ready.at[i, pl.ds(at, rows)],
                    s["rs_send"].at[job, 4 + i],
                    s["rs_recv"].at[job, 4 + i],
                    along(JOBS[job][2][0], k),
                )
            )

    def scatter(job, stage, src, dst):
        axis = JOBS[job][2][stage]
        flight[job] = []
        for k in (1, 2, 3):
            i = 3 + 3 * stage + k - 1
            flight[job].append(
                remote(
                    src.at[(where[axis] + k) % 4],
                    dst.at[k - 1],
                    s["rs_send"].at[job, i],
                    s["rs_recv"].at[job, i],
                    along(axis, k),
                )
            )

    def second_stage(job):
        _, n, axes, _ = JOBS[job]
        arrived(flight[job][2:])
        part, ready = s[f"p{job}"], s[f"v{job}"]
        s["acc1"][:, :n] = part[where[axes[0]]].astype(F32) + ready[0].astype(F32) + ready[1].astype(F32)
        for second in range(4):
            for third in range(4):
                at = second_rows(axes, second, third)
                s["pad2"][9 * third : 9 * third + 9, :n] = s["acc1"][at : at + 9, :n]
            for j in range(n // 128):
                s["ext2"][4 * j : 4 * j + 4] = s["pad2"][32:36, 128 * j : 128 * j + 128]
            s[f"s2_{job}"][second, :, :n] = s["pad2"][0:32, :n].astype(BF16)
            s[f"s2_{job}"][second, :, n:] = s["ext2"][...].astype(BF16)
        scatter(job, 1, s[f"s2_{job}"], s[f"v2_{job}"])

    def total(job, stage, src, dst):
        arrived(flight[job])
        mine = src[where[JOBS[job][2][stage]]].astype(F32)
        return mine + dst[0].astype(F32) + dst[1].astype(F32) + dst[2].astype(F32)

    def third_stage(job):
        n = JOBS[job][1]
        tiles, width = n // 128, third_width(n)
        sums = total(job, 1, s[f"s2_{job}"], s[f"v2_{job}"])
        s["acc2"][0:32, :n] = sums[:, :n]
        s["ext2"][...] = sums[:, n:]
        for j in range(tiles):
            s["acc2"][32:36, 128 * j : 128 * j + 128] = s["ext2"][4 * j : 4 * j + 4]
        for third in range(4):
            for j in range(tiles):
                lanes, at, ninth = slice(128 * j, 128 * j + 128), 128 * (j // 2), 128 * (tiles // 2)
                s["pad3"][8 * (j % 2) : 8 * (j % 2) + 8, at : at + 128] = s["acc2"][9 * third : 9 * third + 8, lanes]
                row = 8 * (tiles % 2) + j
                s["pad3"][row : row + 1, ninth : ninth + 128] = s["acc2"][9 * third + 8 : 9 * third + 9, lanes]
            s[f"s3_{job}"][third] = s["pad3"][:, :width].astype(BF16)
        scatter(job, 2, s[f"s3_{job}"], s[f"v3_{job}"])

    def finish(job):
        first, n, _, _ = JOBS[job]
        tiles, width = n // 128, third_width(n)
        s["pad3"][:, :width] = total(job, 2, s[f"s3_{job}"], s[f"v3_{job}"])
        for j in range(tiles):
            lanes, at, ninth = slice(first + 128 * j, first + 128 * j + 128), 128 * (j // 2), 128 * (tiles // 2)
            row = 8 * (tiles % 2) + j
            gnv_ref[0:8, lanes] = s["pad3"][8 * (j % 2) : 8 * (j % 2) + 8, at : at + 128]
            gnv_ref[8:9, lanes] = s["pad3"][row : row + 1, ninth : ninth + 128]

    for lo in range(0, QKV, 256):
        if lo in (0, 1024):
            loaded(lo // 1024)
        s["qkv1"][:, lo : lo + 256] = nn(s["h1"][...], s["wp"][:, lo : lo + 256]).astype(BF16)
        s["dqkv1"][:, lo : lo + 256] = nn(s["h1"][...], s["wd"][:, lo : lo + 256]).astype(BF16)

    def align_keys(qkv, kx):
        kx[...] = left_64(qkv[:, 512:1152].astype(F32)).astype(BF16)

    row = lax.broadcasted_iota(jnp.int32, (128, 128), 0)
    col = lax.broadcasted_iota(jnp.int32, (128, 128), 1)
    same_frame = row // 8 % 2 == col // 8 % 2
    same_patch = row % 8 == col % 8
    align_keys(s["qkv1"], s["kx1"])
    align_keys(s["dqkv1"], s["dkx"])
    attn_copies = []

    def send_first(out, tan):
        s["attn_s"][:, :, 0:384] = first_part(out).reshape(8, 16, 384)
        s["attn_s"][:, :, 384:768] = first_part(tan).reshape(8, 16, 384)
        attn_copies.extend(frame_exchange(1, s["attn_s"], s["attn_r"]))

    o1, do1 = attend(s["qkv1"], s["dqkv1"], s["kx1"], s["dkx"], s["pn1"], same_frame, FIVE_THREE, send_first)
    s["attn2_s"][:, :, 0:256] = second_part(o1).reshape(8, 16, 256)
    s["attn2_s"][:, :, 256:512] = second_part(do1).reshape(8, 16, 256)
    attn_copies.extend(frame_exchange(4, s["attn2_s"], s["attn2_r"]))

    prepare_left(h1f.astype(BF16).astype(F32), ["h1_z", "h1_y", "h1_x"])

    arrived(clips_copies)
    loaded(2)
    s_out, v_sout = s["wp"][:, S_OUT : S_OUT + OUT], s["wd"][:, S_OUT : S_OUT + OUT]
    clips_p = s["clips_r"][...].reshape(128, D).astype(F32)
    arrived(attn_copies[:7])
    first = s["attn_r"][...].reshape(128, 768)
    first_both = jnp.concatenate([first[:, :384], first[:, 384:]], axis=0)
    through = nt(first_both, s_out[:, :384])
    v_through = nt(first[:, :384], v_sout[:, :384])
    arrived(attn_copies[7:])
    second = s["attn2_r"][...].reshape(128, 512)
    second_both = jnp.concatenate([second[:, :256], second[:, 256:]], axis=0)
    s["r_o1"][0:128, 0:384] = first[:, :384]
    s["r_o1"][0:128, 384:640] = second[:, :256]
    share_right("o1")
    through = through + nt(second_both, s_out[:, 384:])
    v_through = v_through + nt(second[:, :256], v_sout[:, 384:])
    y = (clips_p + through[:128]).astype(BF16).astype(F32)
    dy = (through[128:] + v_through).astype(BF16).astype(F32)
    h2f, rstd = norm_parts(y)
    h2 = h2f.astype(BF16)
    h2_both = jnp.concatenate([h2, norm_tangent(h2f, rstd, dy).astype(BF16)], axis=0)
    prepare_left(h2.astype(F32), ["h2_y", "h2_x"])
    loaded(3)
    for lo in range(0, QKV, 256):
        wp = s["wp"][:, T_QKV + lo : T_QKV + lo + 256]
        wd = s["wd"][:, T_QKV + lo : T_QKV + lo + 256]
        through = nn(h2_both, wp)
        s["qkv2"][:, lo : lo + 256] = through[:128].astype(BF16)
        s["dqkv2"][:, lo : lo + 256] = (through[128:] + nn(h2, wd)).astype(BF16)
    align_keys(s["qkv2"], s["kx2"])
    align_keys(s["dqkv2"], s["dkx"])
    o2, do2 = attend(s["qkv2"], s["dqkv2"], s["kx2"], s["dkx"], s["pn2"], same_patch, ALL)
    o2x = right_64(jnp.concatenate(o2, axis=1)).astype(BF16)
    do2x = right_64(jnp.concatenate(do2, axis=1)).astype(BF16)
    s["r_o2"][0:128, :] = o2x
    share_right("o2")
    loaded(4)
    t_out, v_tout = s["wp"][:, T_OUT : T_OUT + OUT], s["wd"][:, T_OUT : T_OUT + OUT]
    tangent = (dy + nt(do2x, t_out) + nt(o2x, v_tout)).astype(BF16)
    s["tan_s"][...] = tangent.reshape(8, 16, D)
    tan_copies = frame_exchange(3, s["tan_s"], s["tan_r"])
    g = (tangent.astype(F32) * (16384 ** (-0.5))).astype(BF16)
    prepare_left(g.astype(F32), ["g_z", "g_x"])
    s["go"][...] = left_64(nn(g, t_out)).astype(BF16)
    attend_back(s["qkv2"], s["kx2"], s["pn2"], s["go"], s["r_q2"].at[pl.ds(0, 128)], FIVE_THREE, lambda: product(0))
    share_right("q2")
    gq2 = s["r_q2"][0:128, :]
    gh2 = nt(gq2, s["wp"][:, T_QKV : T_QKV + QKV])
    gy = (g.astype(F32) + norm_tangent(h2f, rstd, gh2)).astype(BF16)
    s["go_s"][...] = nn(gy, s_out).astype(BF16).reshape(8, 16, OUT)
    go_copies = frame_exchange(2, s["go_s"], s["go_r"])

    prepare_left(gy.astype(F32), ["gy_z"])
    product(1)
    product(2)
    product(3)
    merge(0)

    arrived(go_copies)
    s["go"][...] = left_64(s["go_r"][...].reshape(128, OUT).astype(F32)).astype(BF16)
    attend_back(s["qkv1"], s["kx1"], s["pn1"], s["go"], s["r_q1"].at[pl.ds(0, 128)], ALL)
    share_right("q1")

    merge(1)
    merge(2)
    merge(3)
    product(4)
    product(5)
    product(6)
    arrived(tan_copies)
    tan = s["tan_r"][...].reshape(128, D).astype(F32)
    for f in range(2):
        tan_ref[f] = jnp.concatenate(
            [tan[16 * t + 8 * f : 16 * t + 8 * f + 8] for t in range(8)], axis=0
        ).astype(BF16)
    second_stage(0)
    second_stage(1)
    second_stage(2)
    second_stage(3)
    for job in (5, 6, 4):
        merge(job)
    for job in (0, 1, 2, 3):
        third_stage(job)
    for job in (5, 6, 4):
        second_stage(job)
    for job in (0, 1, 2, 3):
        finish(job)
    for job in (5, 6, 4):
        third_stage(job)
    for job in (5, 6, 4):
        finish(job)

    for copy in sent:
        copy.wait_send()


def place(tan_in, gnv_in, tan_out, gnv_out):
    tan_out[...] = tan_in[...]
    gnv_out[...] = gnv_in[...]


def body(clips, params, direction):
    tangent, gnv = pl.pallas_call(
        kernel,
        out_shape=(
            jax.ShapeDtypeStruct((2, 64, D), BF16),
            jax.ShapeDtypeStruct((9, 4608), F32),
        ),
        in_specs=[
            pl.BlockSpec(memory_space=pltpu.VMEM),
            pl.BlockSpec(memory_space=pl.ANY),
            pl.BlockSpec(memory_space=pl.ANY),
        ],
        out_specs=(pl.BlockSpec(memory_space=pltpu.VMEM), pl.BlockSpec(memory_space=pltpu.VMEM)),
        scratch_shapes=list(SCRATCH.values()),
        compiler_params=pltpu.CompilerParams(
            collective_id=0, has_side_effects=True, vmem_limit_bytes=62 * 2**20
        ),
    )(clips[0], params, direction)
    tangent, gnv = pl.pallas_call(
        place,
        out_shape=(
            jax.ShapeDtypeStruct((2, 64, D), BF16),
            jax.ShapeDtypeStruct((9, 4608), F32),
        ),
        in_specs=[pl.BlockSpec(memory_space=pltpu.VMEM)] * 2,
        out_specs=(pl.BlockSpec(memory_space=pltpu.VMEM),) * 2,
    )(tangent, gnv)
    return tangent[None], gnv


def solution(mesh):
    in_specs = (P("dp", "frame", None, None), P(), P())
    out_specs = (P("dp", "frame", None, None), P(("dp", "frame"), None))
    return jax.shard_map(body, mesh=mesh, in_specs=in_specs, out_specs=out_specs, check_vma=False)
```

```python
from types import SimpleNamespace

import jax
import jax.numpy as jnp
from jax import lax
from jax.experimental import pallas as pl
from jax.experimental.pallas import tpu as pltpu
from jax.sharding import PartitionSpec as P

MESH = pl.DeviceIdType.MESH
F32 = jnp.float32
BF16 = jnp.bfloat16

D = 1152
HD = 72
HEADS = 8
QKV = 1792
OUT = 640
SCALE = HD ** (-0.5)

S_QKV, S_OUT, T_QKV, T_OUT = 0, 1664, 2304, 3968

HEAD_WINDOWS = [
    (h * HD, (h + 1) * HD, h * HD // 128 * 128, -(-(h + 1) * HD // 128) * 128)
    for h in range(HEADS)
]

ALL = [(0, 1, 2, 3, 4, 5, 6, 7)]
FIVE_THREE = [(0, 1, 2, 3, 4), (5, 6, 7)]

LEFTS = ["g_z", "g_x", "h2_y", "h2_x", "gy_z", "h1_z", "h1_y", "h1_x"]
RIGHTS = {"q1": QKV, "o1": OUT, "q2": QKV, "o2": OUT}

JOBS = [
    (32 * 128, 512, "zxy", [(0, 512, [("g_z", "o2", 128)])]),
    (18 * 128, 896, "yzx", [(0, 896, [("h2_y", "q2", 0)])]),
    (
        25 * 128,
        896,
        "xyz",
        [(0, 768, [("h2_x", "q2", 896)]), (768, 896, [("h2_x", "q2", 1664), ("g_x", "o2", 0)])],
    ),
    (14 * 128, 512, "zxy", [(0, 512, [("gy_z", "o1", 128)])]),
    (
        10 * 128,
        512,
        "zxy",
        [(0, 384, [("h1_z", "q1", 1280)]), (384, 512, [("h1_z", "q1", 1664), ("gy_z", "o1", 0)])],
    ),
    (5 * 128, 640, "yzx", [(0, 640, [("h1_y", "q1", 640)])]),
    (0, 640, "xyz", [(0, 640, [("h1_x", "q1", 0)])]),
]
N_JOBS = len(JOBS)
AT_ONCE = (4, 5, 6)


def third_width(n):
    return (n // 128 + 2) // 2 * 128


def row_moves(order):
    moves = []
    for z in range(4):
        for yh in range(2):
            for c in range(2):
                base = 288 * z + 144 * yh + 72 * c
                if order == "z":
                    moves.append((base, c, 144 * z + 72 * yh, 72))
                    continue
                for x in range(4):
                    if order == "x":
                        moves.append((base + 18 * x, c, 144 * x + 36 * z + 18 * yh, 18))
                        continue
                    for yl in range(2):
                        moves.append((base + 18 * x + 9 * yl, c, 144 * (2 * yh + yl) + 36 * z + 9 * x, 9))
    return moves


def second_rows(axes, second, third):
    if axes == "zxy":
        return 72 * (third // 2) + 18 * second + 9 * (third % 2)
    if axes == "yzx":
        return 36 * second + 9 * third
    return 36 * third + 9 * second


def nn(a, b):
    return jnp.dot(a, b, preferred_element_type=F32)


def nt(a, b):
    return lax.dot_general(a, b, (((1,), (1,)), ((), ())), preferred_element_type=F32)


def tn(a, b):
    return lax.dot_general(a, b, (((0,), (0,)), ((), ())), preferred_element_type=F32)


def left_64(x):
    return pltpu.roll(x, x.shape[1] - 64, 1)


def right_64(x):
    return pltpu.roll(x, 64, 1)


def lane_mask(lo, hi, a, b):
    lane = lax.broadcasted_iota(jnp.int32, (1, b - a), 1) + a
    return (lane >= lo) & (lane < hi)


def add_head(tiles, head, value):
    lo, hi, a, b = HEAD_WINDOWS[head]
    for j in range(a // 128, b // 128):
        piece = value[:, j * 128 - a : (j + 1) * 128 - a]
        mask = lane_mask(lo, hi, j * 128, (j + 1) * 128)
        old = jnp.zeros_like(piece) if tiles[j] is None else tiles[j]
        tiles[j] = jnp.where(mask, piece, old)


def first_part(tiles):
    moved = right_64(jnp.concatenate(tiles[:3], axis=1))
    return jnp.where(lane_mask(64, 384, 0, 384), moved, 0.0).astype(BF16)


def second_part(tiles):
    return left_64(jnp.concatenate(tiles[2:], axis=1))[:, :256].astype(BF16)


def attend(qkv, dqkv, kx, dkx, pn_ref, mask, groups, after_head_4=lambda *_: None):
    out, tan = [None] * 5, [None] * 5
    for group in groups:
        against_k, dk_part, ps = {}, {}, {}
        for h in group:
            lo, hi, a, b = HEAD_WINDOWS[h]
            lanes = jnp.where(lane_mask(lo, hi, a, b), 1.0, 0.0).astype(BF16)
            q = qkv[:, a:b] * lanes
            both = jnp.concatenate([q, dqkv[:, a:b] * lanes], axis=0)
            against_k[h] = nt(both, kx[:, a:b])
            dk_part[h] = nt(q, dkx[:, a:b])
        for h in group:
            e = jnp.where(mask, jnp.exp(against_k[h][:128] * SCALE), 0.0)
            pn = e * (1.0 / jnp.sum(e, axis=1, keepdims=True))
            pn_ref[h] = pn
            ds = (against_k[h][128:] + dk_part[h]) * SCALE
            dp = pn * (ds - jnp.sum(pn * ds, axis=1, keepdims=True))
            ps[h] = jnp.concatenate([pn.astype(BF16), dp.astype(BF16)], axis=0)
        for h in group:
            lo, hi, a, b = HEAD_WINDOWS[h]
            against_v = nn(ps[h], qkv[:, 1152 + a : 1152 + b])
            add_head(out, h, against_v[:128])
            add_head(tan, h, against_v[128:] + nn(ps[h][:128], dqkv[:, 1152 + a : 1152 + b]))
            if h == 4:
                after_head_4(out, tan)
    return out, tan


def attend_back(qkv, kx, pn_ref, go, grad_ref, groups, after_head_4=lambda: None):
    gq, gk, gv = [None] * 5, [None] * 5, [None] * 5
    for group in groups:
        gp, gs, gow = {}, {}, {}
        for h in group:
            lo, hi, a, b = HEAD_WINDOWS[h]
            lanes = jnp.where(lane_mask(lo, hi, a, b), 1.0, 0.0).astype(BF16)
            gow[h] = go[:, a:b]
            gp[h] = nt(gow[h] * lanes, qkv[:, 1152 + a : 1152 + b])
        for h in group:
            pn = pn_ref[h]
            rounded = gp[h].astype(BF16).astype(F32)
            gs[h] = (pn * (rounded - jnp.sum(rounded * pn, axis=1, keepdims=True)) * SCALE).astype(BF16)
        for h in group:
            lo, hi, a, b = HEAD_WINDOWS[h]
            add_head(gv, h, tn(pn_ref[h].astype(BF16), gow[h]))
            add_head(gq, h, nn(gs[h], kx[:, a:b]))
            add_head(gk, h, tn(gs[h], qkv[:, a:b]))
            if h == 4:
                after_head_4()
    gkr = right_64(jnp.concatenate(gk, axis=1))
    for j in range(4):
        grad_ref[:, j * 128 : (j + 1) * 128] = gq[j].astype(BF16)
    grad_ref[:, 512:640] = (gq[4] + gkr[:, :128]).astype(BF16)
    grad_ref[:, 640:1152] = gkr[:, 128:].astype(BF16)
    for j in range(5):
        grad_ref[:, 1152 + j * 128 : 1280 + j * 128] = gv[j].astype(BF16)


def norm_parts(x):
    centred = x - jnp.mean(x, axis=-1, keepdims=True)
    rstd = lax.rsqrt(jnp.mean(centred * centred, axis=-1, keepdims=True) + 1e-06)
    return centred * rstd, rstd


def norm_tangent(normed, rstd, dx):
    return rstd * (
        dx
        - jnp.mean(dx, axis=-1, keepdims=True)
        - normed * jnp.mean(normed * dx, axis=-1, keepdims=True)
    )


def shape_list():
    v = pltpu.VMEM
    dma = pltpu.SemaphoreType.DMA
    scratch = {
        "wp": v((D, 4608), BF16),
        "wd": v((D, 4608), BF16),
        "h1": v((128, D), BF16),
        "qkv1": v((128, QKV), BF16),
        "dqkv1": v((128, QKV), BF16),
        "kx1": v((128, OUT), BF16),
        "dkx": v((128, OUT), BF16),
        "pn1": v((HEADS, 128, 128), F32),
        "qkv2": v((128, QKV), BF16),
        "dqkv2": v((128, QKV), BF16),
        "kx2": v((128, OUT), BF16),
        "pn2": v((HEADS, 128, 128), F32),
        "go": v((128, OUT), BF16),
        "clips_s": v((8, 16, D), BF16),
        "clips_r": v((8, 16, D), BF16),
        "attn_s": v((8, 16, 768), BF16),
        "attn_r": v((8, 16, 768), BF16),
        "attn2_s": v((8, 16, 512), BF16),
        "attn2_r": v((8, 16, 512), BF16),
        "go_s": v((8, 16, OUT), BF16),
        "go_r": v((8, 16, OUT), BF16),
        "tan_s": v((8, 16, D), BF16),
        "tan_r": v((8, 16, D), BF16),
        "lt": v((D, 128), F32),
        "lts": v((2, 576, 128), F32),
        "left": v((len(LEFTS), 576, 256), BF16),
        "left_s": v((len(LEFTS), 576, 128), BF16),
    }
    for name, width in RIGHTS.items():
        scratch["r_" + name] = v((256, width), BF16)
    for i, (_, n, _, _) in enumerate(JOBS):
        scratch["p_%d" % i] = v((4, 144, n), BF16)
        scratch["u_%d" % i] = v((144, n), BF16)
        scratch["m_%d" % i] = v((144, n), BF16)
        scratch["v_%d" % i] = v((3 if i in AT_ONCE else 2, 144, n), BF16)
        scratch["s2_%d" % i] = v((4, 32, n + 128), BF16)
        scratch["v2_%d" % i] = v((3, 32, n + 128), BF16)
        scratch["s3_%d" % i] = v((4, 16, third_width(n)), BF16)
        scratch["v3_%d" % i] = v((3, 16, third_width(n)), BF16)
    scratch["acc1"] = v((144, 896), F32)
    scratch["acc2"] = v((40, 896), F32)
    scratch["pad2"] = v((40, 896), F32)
    scratch["ext2"] = v((32, 128), F32)
    scratch["pad3"] = v((16, 512), F32)
    scratch["w_sem"] = dma((10,))
    scratch["a_send"] = dma((5, 7))
    scratch["a_recv"] = dma((5, 7))
    scratch["c_send"] = dma((len(LEFTS) + len(RIGHTS),))
    scratch["c_recv"] = dma((len(LEFTS) + len(RIGHTS),))
    scratch["rs_send"] = dma((N_JOBS, 12))
    scratch["rs_recv"] = dma((N_JOBS, 12))
    return scratch


SCRATCH = shape_list()


def kernel(clips_ref, params_ref, direction_ref, tan_ref, gnv_ref, *scratch_refs):
    refs = dict(zip(SCRATCH, scratch_refs))
    s = SimpleNamespace(**refs)
    for key in ("p", "u", "m", "v", "s2", "v2", "s3", "v3"):
        setattr(s, key, [refs[key + "_%d" % i] for i in range(N_JOBS)])
    s.rights = {name: refs["r_" + name] for name in RIGHTS}
    dp, fr = lax.axis_index("dp"), lax.axis_index("frame")
    core, y_hi, z = dp % 2, dp // 2 % 2, dp // 4
    x, y_lo = fr // 2, fr % 2
    where = {"z": z, "y": 2 * y_hi + y_lo, "x": x}

    def device(at, c):
        return (at["z"] * 4 + at["y"] // 2 * 2 + c, at["x"] * 2 + at["y"] % 2)

    def along(axis, k):
        at = dict(where)
        at[axis] = (at[axis] + k) % 4
        return device(at, core)

    partner = (dp + 1 - 2 * core, fr)

    def remote(src, dst, send, recv, to):
        copy = pltpu.make_async_remote_copy(
            src_ref=src, dst_ref=dst, send_sem=send, recv_sem=recv, device_id=to, device_id_type=MESH
        )
        copy.start()
        sent.append(copy)
        return copy

    sent = []

    loads = []
    spans = [(0, 1024), (1024, 1792), (1792, 2304), (2304, 4096), (4096, 4608)]
    for i, (lo, hi) in enumerate(spans):
        pair = []
        for j, (src, dst) in enumerate([(params_ref, s.wp), (direction_ref, s.wd)]):
            copy = pltpu.make_async_copy(src.at[:, lo:hi], dst.at[:, lo:hi], s.w_sem.at[2 * i + j])
            copy.start()
            pair.append(copy)
        loads.append(pair)

    def loaded(i):
        for copy in loads[i]:
            copy.wait()

    barrier = pltpu.get_barrier_semaphore()
    peers = [along(axis, k) for axis in "zyx" for k in (1, 2, 3)]
    peers += [(dp, (x + k) % 4 * 2 + 1 - y_lo) for k in (1, 2, 3)]
    peers.append(partner)
    for peer in peers:
        pl.semaphore_signal(barrier, inc=1, device_id=peer, device_id_type=MESH)

    natural = clips_ref[...].astype(F32)
    tokens = jnp.concatenate(
        [natural[f, 8 * t : 8 * t + 8] for t in range(8) for f in range(2)], axis=0
    )
    s.clips_s[...] = tokens.astype(BF16).reshape(8, 16, D)
    h1f, _ = norm_parts(tokens)
    s.h1[...] = h1f.astype(BF16)

    pl.semaphore_wait(barrier, len(peers))

    def frame_exchange(which, src, dst):
        copies = []
        for k in range(1, 8):
            t = (fr + k) % 8
            copies.append(
                remote(src.at[t], dst.at[fr], s.a_send.at[which, k - 1], s.a_recv.at[which, k - 1], (dp, t))
            )
        dst[fr] = src[fr]
        return copies

    def arrived(copies):
        for copy in copies:
            copy.wait_recv()

    clips_copies = frame_exchange(0, s.clips_s, s.clips_r)

    left_copies = {}

    def prepare_left(value, names):
        s.lt[...] = value.T
        for name in names:
            i = LEFTS.index(name)
            for src, c, dst, rows in row_moves(name[-1]):
                s.lts[c, dst : dst + rows, :] = s.lt[src : src + rows, :]
            s.left[i, :, 0:128] = s.lts[core].astype(BF16)
            s.left_s[i] = s.lts[1 - core].astype(BF16)
            left_copies[name] = remote(
                s.left_s.at[i], s.left.at[i, :, pl.ds(128, 128)], s.c_send.at[i], s.c_recv.at[i], partner
            )

    right_copies = {}

    def share_right(name):
        i = len(LEFTS) + list(RIGHTS).index(name)
        ref = s.rights[name]
        right_copies[name] = remote(
            ref.at[pl.ds(0, 128)], ref.at[pl.ds(128, 128)], s.c_send.at[i], s.c_recv.at[i], partner
        )

    s.ext2[...] = jnp.zeros_like(s.ext2)
    s.pad3[...] = jnp.zeros_like(s.pad3)
    flight = {}
    shared = []

    def product(job):
        _, n, axes, segments = JOBS[job]
        needed = [name for _, _, terms in segments for left, right, _ in terms for name in (left, right)]
        for name in needed:
            copies = left_copies if name in left_copies else right_copies
            if name not in shared:
                copies[name].wait_recv()
                shared.append(name)
        part, first_in, ready = s.p[job], s.u[job], s.v[job]
        for lo, hi, terms in segments:
            acc = None
            for left, right, at in terms:
                term = nn(s.left[LEFTS.index(left)], s.rights[right][:, at : at + hi - lo])
                acc = term if acc is None else acc + term
            part[:, :, lo:hi] = acc.astype(BF16).reshape(4, 144, hi - lo)
        here = where[axes[0]]
        if job in AT_ONCE:
            flight[job] = [
                remote(
                    part.at[(here + k) % 4],
                    ready.at[k - 1],
                    s.rs_send.at[job, k - 1],
                    s.rs_recv.at[job, k - 1],
                    along(axes[0], k),
                )
                for k in (2, 1, 3)
            ]
            return
        right, left = along(axes[0], 1), along(axes[0], 3)
        ahead, behind, across = (here + 1) % 4, (here + 3) % 4, (here + 2) % 4
        flight[job] = [
            remote(src.at[pl.ds(at, rows)], dst.at[pl.ds(at, rows)], s.rs_send.at[job, i], s.rs_recv.at[job, i], to)
            for i, (src, dst, at, rows, to) in enumerate(
                [
                    (part.at[across], first_in, 0, 80, right),
                    (part.at[across], first_in, 80, 64, left),
                    (part.at[ahead], ready.at[0], 80, 64, right),
                    (part.at[behind], ready.at[1], 0, 80, left),
                ]
            )
        ]

    def merge(job):
        if job in AT_ONCE:
            return
        here = where[JOBS[job][2][0]]
        part, first_in, merged, ready = s.p[job], s.u[job], s.m[job], s.v[job]
        for i, k, at, rows in [(0, 1, 0, 80), (1, 3, 80, 64)]:
            flight[job][i].wait_recv()
            own = part[(here + k) % 4, at : at + rows].astype(F32)
            merged[at : at + rows] = (own + first_in[at : at + rows].astype(F32)).astype(BF16)
            flight[job].append(
                remote(
                    merged.at[pl.ds(at, rows)],
                    ready.at[i, pl.ds(at, rows)],
                    s.rs_send.at[job, 4 + i],
                    s.rs_recv.at[job, 4 + i],
                    along(JOBS[job][2][0], k),
                )
            )

    def scatter(job, stage, src, dst):
        axis = JOBS[job][2][stage]
        flight[job] = []
        for k in (1, 2, 3):
            i = 3 + 3 * stage + k - 1
            flight[job].append(
                remote(
                    src.at[(where[axis] + k) % 4],
                    dst.at[k - 1],
                    s.rs_send.at[job, i],
                    s.rs_recv.at[job, i],
                    along(axis, k),
                )
            )

    def second_stage(job):
        _, n, axes, _ = JOBS[job]
        arrived(flight[job] if job in AT_ONCE else flight[job][2:])
        part, ready = s.p[job], s.v[job]
        acc = part[where[axes[0]]].astype(F32) + ready[0].astype(F32) + ready[1].astype(F32)
        s.acc1[:, :n] = acc + ready[2].astype(F32) if job in AT_ONCE else acc
        for second in range(4):
            for third in range(4):
                at = second_rows(axes, second, third)
                s.pad2[9 * third : 9 * third + 9, :n] = s.acc1[at : at + 9, :n]
            for j in range(n // 128):
                s.ext2[4 * j : 4 * j + 4] = s.pad2[32:36, 128 * j : 128 * j + 128]
            s.s2[job][second, :, :n] = s.pad2[0:32, :n].astype(BF16)
            s.s2[job][second, :, n:] = s.ext2[...].astype(BF16)
        scatter(job, 1, s.s2[job], s.v2[job])

    def total(job, stage, src, dst):
        arrived(flight[job])
        mine = src[where[JOBS[job][2][stage]]].astype(F32)
        return mine + dst[0].astype(F32) + dst[1].astype(F32) + dst[2].astype(F32)

    def third_stage(job):
        n = JOBS[job][1]
        tiles, width = n // 128, third_width(n)
        sums = total(job, 1, s.s2[job], s.v2[job])
        s.acc2[0:32, :n] = sums[:, :n]
        s.ext2[...] = sums[:, n:]
        for j in range(tiles):
            s.acc2[32:36, 128 * j : 128 * j + 128] = s.ext2[4 * j : 4 * j + 4]
        for third in range(4):
            for j in range(tiles):
                lanes, at, ninth = slice(128 * j, 128 * j + 128), 128 * (j // 2), 128 * (tiles // 2)
                s.pad3[8 * (j % 2) : 8 * (j % 2) + 8, at : at + 128] = s.acc2[9 * third : 9 * third + 8, lanes]
                row = 8 * (tiles % 2) + j
                s.pad3[row : row + 1, ninth : ninth + 128] = s.acc2[9 * third + 8 : 9 * third + 9, lanes]
            s.s3[job][third] = s.pad3[:, :width].astype(BF16)
        scatter(job, 2, s.s3[job], s.v3[job])

    def finish(job):
        first, n, _, _ = JOBS[job]
        tiles, width = n // 128, third_width(n)
        s.pad3[:, :width] = total(job, 2, s.s3[job], s.v3[job])
        for j in range(tiles):
            lanes, at, ninth = slice(first + 128 * j, first + 128 * j + 128), 128 * (j // 2), 128 * (tiles // 2)
            row = 8 * (tiles % 2) + j
            gnv_ref[0:8, lanes] = s.pad3[8 * (j % 2) : 8 * (j % 2) + 8, at : at + 128]
            gnv_ref[8:9, lanes] = s.pad3[row : row + 1, ninth : ninth + 128]

    for lo in range(0, QKV, 256):
        if lo in (0, 1024):
            loaded(lo // 1024)
        s.qkv1[:, lo : lo + 256] = nn(s.h1[...], s.wp[:, lo : lo + 256]).astype(BF16)
        s.dqkv1[:, lo : lo + 256] = nn(s.h1[...], s.wd[:, lo : lo + 256]).astype(BF16)

    def align_keys(qkv, kx):
        kx[...] = left_64(qkv[:, 512:1152].astype(F32)).astype(BF16)

    row = lax.broadcasted_iota(jnp.int32, (128, 128), 0)
    col = lax.broadcasted_iota(jnp.int32, (128, 128), 1)
    same_frame = row // 8 % 2 == col // 8 % 2
    same_patch = row % 8 == col % 8
    align_keys(s.qkv1, s.kx1)
    align_keys(s.dqkv1, s.dkx)
    attn_copies = []

    def send_first(out, tan):
        s.attn_s[:, :, 0:384] = first_part(out).reshape(8, 16, 384)
        s.attn_s[:, :, 384:768] = first_part(tan).reshape(8, 16, 384)
        attn_copies.extend(frame_exchange(1, s.attn_s, s.attn_r))

    o1, do1 = attend(s.qkv1, s.dqkv1, s.kx1, s.dkx, s.pn1, same_frame, FIVE_THREE, send_first)
    s.attn2_s[:, :, 0:256] = second_part(o1).reshape(8, 16, 256)
    s.attn2_s[:, :, 256:512] = second_part(do1).reshape(8, 16, 256)
    attn_copies.extend(frame_exchange(4, s.attn2_s, s.attn2_r))

    prepare_left(h1f.astype(BF16).astype(F32), ["h1_z", "h1_y", "h1_x"])

    arrived(clips_copies)
    loaded(2)
    s_out, v_sout = s.wp[:, S_OUT : S_OUT + OUT], s.wd[:, S_OUT : S_OUT + OUT]
    clips_p = s.clips_r[...].reshape(128, D).astype(F32)
    arrived(attn_copies[:7])
    first = s.attn_r[...].reshape(128, 768)
    first_both = jnp.concatenate([first[:, :384], first[:, 384:]], axis=0)
    through = nt(first_both, s_out[:, :384])
    v_through = nt(first[:, :384], v_sout[:, :384])
    arrived(attn_copies[7:])
    second = s.attn2_r[...].reshape(128, 512)
    second_both = jnp.concatenate([second[:, :256], second[:, 256:]], axis=0)
    s.r_o1[0:128, 0:384] = first[:, :384]
    s.r_o1[0:128, 384:640] = second[:, :256]
    share_right("o1")
    through = through + nt(second_both, s_out[:, 384:])
    v_through = v_through + nt(second[:, :256], v_sout[:, 384:])
    y = (clips_p + through[:128]).astype(BF16).astype(F32)
    dy = (through[128:] + v_through).astype(BF16).astype(F32)
    h2f, rstd = norm_parts(y)
    h2 = h2f.astype(BF16)
    h2_both = jnp.concatenate([h2, norm_tangent(h2f, rstd, dy).astype(BF16)], axis=0)
    prepare_left(h2.astype(F32), ["h2_y", "h2_x"])
    loaded(3)
    for lo in range(0, QKV, 256):
        wp = s.wp[:, T_QKV + lo : T_QKV + lo + 256]
        wd = s.wd[:, T_QKV + lo : T_QKV + lo + 256]
        through = nn(h2_both, wp)
        s.qkv2[:, lo : lo + 256] = through[:128].astype(BF16)
        s.dqkv2[:, lo : lo + 256] = (through[128:] + nn(h2, wd)).astype(BF16)
    align_keys(s.qkv2, s.kx2)
    align_keys(s.dqkv2, s.dkx)
    o2, do2 = attend(s.qkv2, s.dqkv2, s.kx2, s.dkx, s.pn2, same_patch, ALL)
    o2x = right_64(jnp.concatenate(o2, axis=1)).astype(BF16)
    do2x = right_64(jnp.concatenate(do2, axis=1)).astype(BF16)
    s.r_o2[0:128, :] = o2x
    share_right("o2")
    loaded(4)
    t_out, v_tout = s.wp[:, T_OUT : T_OUT + OUT], s.wd[:, T_OUT : T_OUT + OUT]
    tangent = (dy + nt(do2x, t_out) + nt(o2x, v_tout)).astype(BF16)
    s.tan_s[...] = tangent.reshape(8, 16, D)
    tan_copies = frame_exchange(3, s.tan_s, s.tan_r)
    g = (tangent.astype(F32) * (16384 ** (-0.5))).astype(BF16)
    prepare_left(g.astype(F32), ["g_z", "g_x"])
    s.go[...] = left_64(nn(g, t_out)).astype(BF16)
    attend_back(s.qkv2, s.kx2, s.pn2, s.go, s.r_q2.at[pl.ds(0, 128)], FIVE_THREE, lambda: product(0))
    share_right("q2")
    gq2 = s.r_q2[0:128, :]
    gh2 = nt(gq2, s.wp[:, T_QKV : T_QKV + QKV])
    gy = (g.astype(F32) + norm_tangent(h2f, rstd, gh2)).astype(BF16)
    s.go_s[...] = nn(gy, s_out).astype(BF16).reshape(8, 16, OUT)
    go_copies = frame_exchange(2, s.go_s, s.go_r)

    prepare_left(gy.astype(F32), ["gy_z"])
    product(1)
    product(2)
    product(3)
    merge(0)

    arrived(go_copies)
    s.go[...] = left_64(s.go_r[...].reshape(128, OUT).astype(F32)).astype(BF16)
    attend_back(s.qkv1, s.kx1, s.pn1, s.go, s.r_q1.at[pl.ds(0, 128)], ALL)
    share_right("q1")

    merge(1)
    merge(2)
    merge(3)
    product(4)
    product(5)
    product(6)
    second_stage(0)
    second_stage(1)
    second_stage(2)
    second_stage(3)
    for job in (5, 6, 4):
        merge(job)
    for job in (5, 6, 4):
        second_stage(job)
    for job in (0, 1, 2, 3):
        third_stage(job)
    for job in (5, 6, 4):
        third_stage(job)
    arrived(tan_copies)
    tan = s.tan_r[...].reshape(128, D).astype(F32)
    for f in range(2):
        tan_ref[f] = jnp.concatenate(
            [tan[16 * t + 8 * f : 16 * t + 8 * f + 8] for t in range(8)], axis=0
        ).astype(BF16)
    for job in (0, 1, 2, 3):
        finish(job)
    for job in (5, 6, 4):
        finish(job)

    for copy in sent:
        copy.wait_send()


def place(tan_in, gnv_in, tan_out, gnv_out):
    tan_out[...] = tan_in[...]
    gnv_out[...] = gnv_in[...]


def body(clips, params, direction):
    tangent, gnv = pl.pallas_call(
        kernel,
        out_shape=(
            jax.ShapeDtypeStruct((2, 64, D), BF16),
            jax.ShapeDtypeStruct((9, 4608), F32),
        ),
        in_specs=[
            pl.BlockSpec(memory_space=pltpu.VMEM),
            pl.BlockSpec(memory_space=pl.ANY),
            pl.BlockSpec(memory_space=pl.ANY),
        ],
        out_specs=(pl.BlockSpec(memory_space=pltpu.VMEM), pl.BlockSpec(memory_space=pltpu.VMEM)),
        scratch_shapes=list(SCRATCH.values()),
        compiler_params=pltpu.CompilerParams(
            collective_id=0, has_side_effects=True, vmem_limit_bytes=62 * 2**20
        ),
    )(clips[0], params, direction)
    tangent, gnv = pl.pallas_call(
        place,
        out_shape=(
            jax.ShapeDtypeStruct((2, 64, D), BF16),
            jax.ShapeDtypeStruct((9, 4608), F32),
        ),
        in_specs=[pl.BlockSpec(memory_space=pltpu.VMEM)] * 2,
        out_specs=(pl.BlockSpec(memory_space=pltpu.VMEM),) * 2,
    )(tangent, gnv)
    return tangent[None], gnv


def solution(mesh):
    in_specs = (P("dp", "frame", None, None), P(), P())
    out_specs = (P("dp", "frame", None, None), P(("dp", "frame"), None))
    return jax.shard_map(body, mesh=mesh, in_specs=in_specs, out_specs=out_specs, check_vma=False)
```
